256 devices in a mesh: col: 64 (over z, y_hi, x), row: 4 (over y_lo, core).
Axes of the slice: x: 4, y: 4 (y_hi: 2, y_lo: 2; y = y_hi * 2 + y_lo), z: 8, core: 2. Of those that a mesh axis runs over, the one named last changes fastest.
Arguments:
- matrix: float32 [16384, 8192], P('row', 'col'), may hold values from -40 to 40
- active: int32 [2, 32], replicated, may hold values 0 or 1
Outputs:
- rotated: float32 [16384, 8192], P('row', 'col')
The draws below stay inside these ranges and needn't reach their ends.
All inputs are finite; a program needn't handle non-finite values.
Results may differ from the reference program's by a relative error of at most 0.00012.
Values sent between devices are 32-bit elements; how exact they have to be, the bound alone decides.
A program may use at most 64 MiB of HBM per device.

```python
import math
import jax
import jax.numpy as jnp
from jax import lax

BLK = 128
STEPS = 2
ROWS = 16384
COLS = 8192
NPAIR = 32


def draw_matrix(key, part):
    key = jax.random.fold_in(key, 11)
    key_values, key_rows, key_cols = jax.random.split(key, 3)
    values = jax.random.normal(key_values, (ROWS, COLS), jnp.float32)
    row_low, row_high, col_low, col_high = (0.5, 2.0, 0.3, 3.0)
    row_scale = jnp.exp(jax.random.uniform(key_rows, (ROWS, 1), jnp.float32, math.log(row_low), math.log(row_high)))
    col_scale = jnp.exp(jax.random.uniform(key_cols, (1, COLS), jnp.float32, math.log(col_low), math.log(col_high)))
    return values * row_scale * col_scale


def touch_ends(drawn, own_key, low, largest):
    spot = [jax.random.randint(jax.random.fold_in(own_key, axis), (), 0, length) for axis, length in enumerate(drawn.shape)]
    main_axis = drawn.shape.index(max(drawn.shape))
    neighbour = spot[:main_axis] + [(spot[main_axis] + 1) % drawn.shape[main_axis]] + spot[main_axis + 1:]
    return drawn.at[tuple(spot)].set(low).at[tuple(neighbour)].set(largest)


def setup_inputs(seed: int = 0) -> dict:
    keys = jax.random.split(jax.random.key(seed), 3)
    matrix = draw_matrix(jax.random.fold_in(keys[2], 71), 0)
    active = touch_ends((jax.random.randint(keys[1], (STEPS, NPAIR), 0, 4) < 3).astype(jnp.int32), jax.random.fold_in(keys[1], 1), 0, 1)
    return dict(matrix=matrix, active=active)


def inverse_spd(matrix_in):
    order = matrix_in.shape[-1]
    factor = jnp.linalg.cholesky(matrix_in)
    identity = jnp.broadcast_to(jnp.eye(order, dtype=matrix_in.dtype), matrix_in.shape)
    solved = lax.linalg.triangular_solve(factor, identity, left_side=True, lower=True)
    return lax.linalg.triangular_solve(factor, solved, left_side=True, lower=True, transpose_a=True)

def rotation(gram_upper, gram_cross, gram_lower, active_flag, total_rows):
    width_block = gram_upper.shape[-1]
    scale_upper = 1.0 / jnp.sqrt(jnp.diagonal(gram_upper, axis1=-2, axis2=-1) / total_rows + 1e-06)
    scale_lower = 1.0 / jnp.sqrt(jnp.diagonal(gram_lower, axis1=-2, axis2=-1) / total_rows + 1e-06)
    coupling = 0.25 / math.sqrt(total_rows * width_block) * scale_upper[..., :, None] * gram_cross * scale_lower[..., None, :]
    coupling_t = jnp.swapaxes(coupling, -1, -2)
    outer_left = jnp.matmul(coupling, coupling_t, precision=lax.Precision.HIGHEST)
    outer_right = jnp.matmul(coupling_t, coupling, precision=lax.Precision.HIGHEST)
    identity = jnp.eye(width_block, dtype=gram_upper.dtype)
    inv_left = inverse_spd(identity + outer_left)
    inv_right = inverse_spd(identity + outer_right)
    upper_left = jnp.matmul(identity - outer_left, inv_left, precision=lax.Precision.HIGHEST)
    upper_right = 2.0 * jnp.matmul(coupling, inv_right, precision=lax.Precision.HIGHEST)
    lower_left = -2.0 * jnp.matmul(coupling_t, inv_left, precision=lax.Precision.HIGHEST)
    lower_right = jnp.matmul(identity - outer_right, inv_right, precision=lax.Precision.HIGHEST)
    rotor = jnp.concatenate([jnp.concatenate([upper_left, upper_right], axis=-1), jnp.concatenate([lower_left, lower_right], axis=-1)], axis=-2)
    identity_pair = jnp.eye(2 * width_block, dtype=gram_upper.dtype)
    return jnp.where(active_flag[..., None, None] == 1, rotor, identity_pair)

def reference(matrix, active):
    blocks = matrix.reshape(ROWS, NPAIR, 2, BLK)
    upper_blocks = blocks[:, :, 0, :]
    lower_blocks = blocks[:, :, 1, :]
    for section_index in range(STEPS):
        gram_upper = jnp.einsum('rki,rkj->kij', upper_blocks, upper_blocks, precision=lax.Precision.HIGHEST)
        gram_cross = jnp.einsum('rki,rkj->kij', upper_blocks, lower_blocks, precision=lax.Precision.HIGHEST)
        gram_lower = jnp.einsum('rki,rkj->kij', lower_blocks, lower_blocks, precision=lax.Precision.HIGHEST)
        rotor = rotation(gram_upper, gram_cross, gram_lower, active[section_index], ROWS)
        paired = jnp.concatenate([upper_blocks, lower_blocks], axis=2)
        turned = jnp.einsum('rki,kij->rkj', paired, rotor, precision=lax.Precision.HIGHEST)
        new_upper = turned[:, :, :BLK]
        new_lower = turned[:, :, BLK:]
        upper_blocks = jnp.concatenate([new_lower[:, -1:], new_lower[:, :-1]], axis=1)
        lower_blocks = new_upper
    return jnp.stack([upper_blocks, lower_blocks], axis=2).reshape(ROWS, COLS)
```

```python
import functools
import math

import jax
import jax.numpy as jnp
from jax import lax
from jax.experimental import pallas as pl
from jax.experimental.pallas import tpu as pltpu
from jax.sharding import PartitionSpec as P

MESH = pl.DeviceIdType.MESH
CHUNK = 256
BLOCK = 4


def lane_spread(value, lane):
    return jnp.broadcast_to(value[:, lane : lane + 1], value.shape)


def eliminate(matrix_in, first):
    order = matrix_in.shape[0]
    lane = lax.broadcasted_iota(jnp.int32, (8, order), 1)
    row = lax.broadcasted_iota(jnp.int32, (8, order), 0)
    lane_all = lax.broadcasted_iota(jnp.int32, (order, order), 1)
    tiles = order // 8
    pivots = range(first, first + BLOCK)
    rows = [jnp.broadcast_to(matrix_in[p : p + 1], (8, order)) for p in pivots]
    small = [[lane_spread(rows[i], p) for p in pivots] for i in range(BLOCK)]
    columns = [lane_spread(matrix_in, p) for p in pivots]
    result = matrix_in
    for i, p in enumerate(pivots):
        inverse = 1.0 / small[i][i]
        scaled = jnp.where(lane == p, inverse, rows[i] * inverse)
        ratio = [small[i][k] * inverse for k in range(BLOCK)]
        scaled_all = jnp.concatenate([scaled] * tiles, axis=0)
        result = jnp.where(lane_all == p, 0.0, result) - columns[i] * scaled_all
        result = jnp.concatenate([jnp.where(row == p, scaled, result[:8]), result[8:]], axis=0)
        for k in range(i + 1, BLOCK):
            ratio_all = jnp.concatenate([ratio[k]] * tiles, axis=0)
            updated = columns[k] - columns[i] * ratio_all
            columns[k] = jnp.concatenate([jnp.where(row == p, ratio[k], updated[:8]), updated[8:]], axis=0)
            rows[k] = jnp.where(lane == p, 0.0, rows[k]) - small[k][i] * scaled
        for k in range(i + 1, BLOCK):
            small[k] = [small[k][j] - small[k][i] * ratio[j] if j > i else small[k][j] for j in range(BLOCK)]
    return result


def inverse_spd(matrix_in):
    order = matrix_in.shape[0]

    def body(_, value):
        for first in range(0, 8, BLOCK):
            value = eliminate(value, first)
        value = jnp.concatenate([value[8:], value[:8]], axis=0)
        return pltpu.roll(value, order - 8, 1)

    return lax.fori_loop(0, order // 8, body, matrix_in)


def split(value):
    high = value.astype(jnp.bfloat16)
    return high, (value - high.astype(jnp.float32)).astype(jnp.bfloat16)


def exact_dot(left, right, left_dim=1, right_dim=0):
    return lax.dot_general(
        left,
        right,
        (((left_dim,), (right_dim,)), ((), ())),
        precision=lax.Precision.HIGHEST,
        preferred_element_type=jnp.float32,
    )


def rotor_of(gram, flag, total_rows):
    width = gram.shape[1]
    scale_upper = 1.0 / jnp.sqrt(jnp.sum(gram[width : width + 8], axis=0, keepdims=True) / total_rows + 1e-06)
    scale_lower = 1.0 / jnp.sqrt(jnp.sum(gram[width + 8 :], axis=0, keepdims=True) / total_rows + 1e-06)
    scale_rows = jnp.broadcast_to(scale_upper, (width, width)).T
    coupling = 0.25 / math.sqrt(total_rows * width) * flag * scale_rows * gram[:width] * scale_lower
    row = lax.broadcasted_iota(jnp.int32, (width, width), 0)
    lane = lax.broadcasted_iota(jnp.int32, (width, width), 1)
    identity = jnp.where(row == lane, 1.0, 0.0)
    inv_left = inverse_spd(identity + exact_dot(coupling, coupling, 1, 1))
    product = exact_dot(inv_left, coupling)
    lower_right = identity - 2.0 * exact_dot(coupling, product, 0, 0)
    top = jnp.concatenate([2.0 * inv_left - identity, 2.0 * product], axis=1)
    bottom = jnp.concatenate([-2.0 * product.T, lower_right], axis=1)
    return jnp.concatenate([top, bottom], axis=0)


def kernel(
    total_rows, col_count, matrix_ref, active_ref, out_ref,
    first, second, sending, result, gram, norms, shared, arrived, rotor_parts,
    own_sem, a_send, a_recv, b_send, b_recv, g_send, g_recv, c_send, c_recv, local_sem,
):
    col, row = lax.axis_index("col"), lax.axis_index("row")
    odd = lax.rem(col, 2)
    pair = col // 2
    parity = lax.rem(pair, 2)
    half = lax.rem(odd + parity, 2)
    width = matrix_ref.shape[1]
    half_rows = matrix_ref.shape[0] // 2
    chunks = half_rows // CHUNK
    upper_col = 2 * pair

    def wrapped(position):
        return lax.rem(position + col_count, col_count)

    partner = (col + 1 - 2 * odd, row)
    sibling = (col, row + 1 - 2 * lax.rem(row, 2))
    beside = (col, lax.rem(row + 2, 4))
    b_target = (wrapped(upper_col + 3 - odd), row)
    b_source = (wrapped(upper_col - 1 - odd), row)
    next_upper = (wrapped(upper_col + 2), row)
    last_upper = (wrapped(upper_col - 2), row)

    barrier = pltpu.get_barrier_semaphore()
    for device in (partner, sibling, beside, b_target, b_source):
        pl.semaphore_signal(barrier, inc=1, device_id=device, device_id_type=MESH)

    @pl.when(odd == 0)
    def _():
        for device in (next_upper, last_upper):
            pl.semaphore_signal(barrier, inc=1, device_id=device, device_id_type=MESH)

    pl.semaphore_wait(barrier, 7 - 2 * odd)

    def rows_of(which, chunk):
        return pl.ds(pl.multiple_of(which * half_rows + chunk * CHUNK, CHUNK), CHUNK)

    def a_copy(chunk):
        return pltpu.make_async_remote_copy(
            src_ref=matrix_ref.at[rows_of(1 - half, chunk)],
            dst_ref=first.at[odd, rows_of(0, chunk)],
            send_sem=a_send.at[chunk],
            recv_sem=a_recv.at[chunk],
            device_id=partner,
            device_id_type=MESH,
        )

    def b_copy(chunk):
        return pltpu.make_async_remote_copy(
            src_ref=sending.at[rows_of(0, chunk)],
            dst_ref=second.at[0, rows_of(0, chunk)],
            send_sem=b_send.at[chunk],
            recv_sem=b_recv.at[chunk],
            device_id=b_target,
            device_id_type=MESH,
        )

    def c_copy(side, chunk, origin, device):
        return pltpu.make_async_remote_copy(
            src_ref=result.at[side, rows_of(0, chunk)],
            dst_ref=out_ref.at[rows_of(half, chunk)],
            send_sem=c_send.at[side, chunk],
            recv_sem=c_recv.at[origin, chunk],
            device_id=device,
            device_id_type=MESH,
        )

    def c_upper(chunk):
        return c_copy(0, chunk, 0, partner)

    def c_lower(chunk):
        return c_copy(1, chunk, odd, next_upper)

    def c_local(chunk):
        return pltpu.make_async_copy(
            result.at[0, rows_of(0, chunk)], out_ref.at[rows_of(half, chunk)], local_sem.at[chunk]
        )

    def each_chunk(body):
        lax.fori_loop(0, chunks, lambda chunk, carry: (body(chunk), carry)[1], 0)

    own = pltpu.make_async_copy(
        matrix_ref.at[pl.ds(pl.multiple_of(half * half_rows, CHUNK), half_rows)], first.at[odd], own_sem
    )
    each_chunk(lambda chunk: a_copy(chunk).start())
    own.start()

    def clear():
        gram[...] = jnp.zeros_like(gram)
        norms[...] = jnp.zeros_like(norms)

    def add_gram(held, chunk):
        upper = held[0, rows_of(0, chunk)]
        lower = held[1, rows_of(0, chunk)]
        gram[...] += lax.dot_general(
            jnp.concatenate(split(upper), axis=1),
            jnp.concatenate(split(lower), axis=1),
            (((0,), (0,)), ((), ())),
            preferred_element_type=jnp.float32,
        )
        norms[0] += jnp.sum((upper * upper).reshape(CHUNK // 8, 8, width), axis=0)
        norms[1] += jnp.sum((lower * lower).reshape(CHUNK // 8, 8, width), axis=0)

    def make_rotor(step):
        shared[step, 0, :width] = (gram[:width, :width] + gram[width:, width:]) + (
            gram[:width, width:] + gram[width:, :width]
        )
        shared[step, 0, width : width + 8] = norms[0]
        shared[step, 0, width + 8 :] = norms[1]
        for stage, device in enumerate((sibling, beside, partner)):
            copy = pltpu.make_async_remote_copy(
                src_ref=shared.at[step, stage],
                dst_ref=arrived.at[step, stage],
                send_sem=g_send.at[step, stage],
                recv_sem=g_recv.at[step, stage],
                device_id=device,
                device_id_type=MESH,
            )
            copy.start()
            copy.wait()
            shared[step, stage + 1] = shared[step, stage] + arrived[step, stage]
        flag = active_ref[step, pair].astype(jnp.float32)
        high, low = split(rotor_of(shared[step, 3], flag, total_rows))
        rotor_parts[: 2 * width] = high
        rotor_parts[2 * width : 4 * width] = high
        rotor_parts[4 * width :] = low

    def turned(held, chunk):
        paired = jnp.concatenate([held[0, rows_of(0, chunk)], held[1, rows_of(0, chunk)]], axis=1)
        high, low = split(paired)
        return jnp.dot(
            jnp.concatenate([high, low, high], axis=1), rotor_parts[...], preferred_element_type=jnp.float32
        )

    clear()
    own.wait()

    def gather_first(chunk):
        a_copy(chunk).wait_recv()
        add_gram(first, chunk)

    each_chunk(gather_first)
    make_rotor(0)

    def turn_first(chunk):
        value = turned(first, chunk)
        sending[rows_of(0, chunk)] = value[:, width:]
        b_copy(chunk).start()
        second[1, rows_of(0, chunk)] = value[:, :width]

    each_chunk(turn_first)
    clear()

    def gather_second(chunk):
        b_copy(chunk).wait_recv()
        add_gram(second, chunk)

    each_chunk(gather_second)
    make_rotor(1)

    def turn_second(chunk):
        value = turned(second, chunk)
        result[1, rows_of(0, chunk)] = value[:, width:]
        c_lower(chunk).start()
        result[0, rows_of(0, chunk)] = value[:, :width]

        @pl.when(odd == 0)
        def _():
            c_upper(chunk).start()

        @pl.when(odd == 1)
        def _():
            c_local(chunk).start()

    each_chunk(turn_second)

    def finish(chunk):
        a_copy(chunk).wait_send()
        b_copy(chunk).wait_send()
        c_lower(chunk).wait_send()
        c_copy(0, chunk, 0, partner).wait_recv()

        @pl.when(odd == 0)
        def _():
            c_upper(chunk).wait_send()
            c_copy(0, chunk, 1, partner).wait_recv()

        @pl.when(odd == 1)
        def _():
            c_local(chunk).wait()

    each_chunk(finish)


def solution(mesh):
    col_count = mesh.shape["col"]

    def on_device(matrix, active):
        rows, width = matrix.shape
        half_rows = rows // 2
        chunks = half_rows // CHUNK
        total_rows = rows * mesh.shape["row"]
        payload = width + 16
        dma = pltpu.SemaphoreType.DMA
        return pl.pallas_call(
            functools.partial(kernel, total_rows, col_count),
            out_shape=jax.ShapeDtypeStruct(matrix.shape, jnp.float32),
            in_specs=[pl.BlockSpec(memory_space=pl.ANY), pl.BlockSpec(memory_space=pltpu.SMEM)],
            out_specs=pl.BlockSpec(memory_space=pl.ANY),
            scratch_shapes=[
                pltpu.VMEM((2, half_rows, width), jnp.float32),
                pltpu.VMEM((2, half_rows, width), jnp.float32),
                pltpu.VMEM((half_rows, width), jnp.float32),
                pltpu.VMEM((2, half_rows, width), jnp.float32),
                pltpu.VMEM((2 * width, 2 * width), jnp.float32),
                pltpu.VMEM((2, 8, width), jnp.float32),
                pltpu.VMEM((2, 4, payload, width), jnp.float32),
                pltpu.VMEM((2, 3, payload, width), jnp.float32),
                pltpu.VMEM((6 * width, 2 * width), jnp.bfloat16),
                dma(()),
                dma((chunks,)),
                dma((chunks,)),
                dma((chunks,)),
                dma((chunks,)),
                dma((2, 3)),
                dma((2, 3)),
                dma((2, chunks)),
                dma((2, chunks)),
                dma((chunks,)),
            ],
            compiler_params=pltpu.CompilerParams(
                collective_id=0, has_side_effects=True, vmem_limit_bytes=40 * 2**20
            ),
            name="tournament",
        )(matrix, active)

    return jax.shard_map(
        on_device, mesh=mesh, in_specs=(P("row", "col"), P()), out_specs=P("row", "col"), check_vma=False
    )
```

```python
import functools
import math

import jax
import jax.numpy as jnp
from jax import lax
from jax.experimental import pallas as pl
from jax.experimental.pallas import tpu as pltpu
from jax.sharding import PartitionSpec as P

MESH = pl.DeviceIdType.MESH
CHUNK = 256
BLOCK = 4


def lane_spread(value, lane):
    return jnp.broadcast_to(value[:, lane : lane + 1], value.shape)


def eliminate(matrix_in, first):
    order = matrix_in.shape[0]
    lane = lax.broadcasted_iota(jnp.int32, (8, order), 1)
    row = lax.broadcasted_iota(jnp.int32, (8, order), 0)
    lane_all = lax.broadcasted_iota(jnp.int32, (order, order), 1)
    tiles = order // 8
    pivots = range(first, first + BLOCK)
    rows = [jnp.broadcast_to(matrix_in[p : p + 1], (8, order)) for p in pivots]
    small = [[lane_spread(rows[i], p) for p in pivots] for i in range(BLOCK)]
    columns = [lane_spread(matrix_in, p) for p in pivots]
    result = matrix_in
    for i, p in enumerate(pivots):
        inverse = 1.0 / small[i][i]
        scaled = jnp.where(lane == p, inverse, rows[i] * inverse)
        ratio = [small[i][k] * inverse for k in range(BLOCK)]
        scaled_all = jnp.concatenate([scaled] * tiles, axis=0)
        result = jnp.where(lane_all == p, 0.0, result) - columns[i] * scaled_all
        result = jnp.concatenate([jnp.where(row == p, scaled, result[:8]), result[8:]], axis=0)
        for k in range(i + 1, BLOCK):
            ratio_all = jnp.concatenate([ratio[k]] * tiles, axis=0)
            updated = columns[k] - columns[i] * ratio_all
            columns[k] = jnp.concatenate([jnp.where(row == p, ratio[k], updated[:8]), updated[8:]], axis=0)
            rows[k] = jnp.where(lane == p, 0.0, rows[k]) - small[k][i] * scaled
        for k in range(i + 1, BLOCK):
            small[k] = [small[k][j] - small[k][i] * ratio[j] if j > i else small[k][j] for j in range(BLOCK)]
    return result


def inverse_spd(matrix_in):
    order = matrix_in.shape[0]

    def body(_, value):
        for first in range(0, 8, BLOCK):
            value = eliminate(value, first)
        value = jnp.concatenate([value[8:], value[:8]], axis=0)
        return pltpu.roll(value, order - 8, 1)

    return lax.fori_loop(0, order // 8, body, matrix_in)


def split(value):
    high = value.astype(jnp.bfloat16)
    return high, (value - high.astype(jnp.float32)).astype(jnp.bfloat16)


def exact_dot(left, right, left_dim=1, right_dim=0):
    return lax.dot_general(
        left,
        right,
        (((left_dim,), (right_dim,)), ((), ())),
        precision=lax.Precision.HIGHEST,
        preferred_element_type=jnp.float32,
    )


def rotor_of(gram, flag, total_rows):
    width = gram.shape[1]
    scale_upper = 1.0 / jnp.sqrt(jnp.sum(gram[width : width + 8], axis=0, keepdims=True) / total_rows + 1e-06)
    scale_lower = 1.0 / jnp.sqrt(jnp.sum(gram[width + 8 :], axis=0, keepdims=True) / total_rows + 1e-06)
    scale_rows = jnp.broadcast_to(scale_upper, (width, width)).T
    coupling = 0.25 / math.sqrt(total_rows * width) * flag * scale_rows * gram[:width] * scale_lower
    row = lax.broadcasted_iota(jnp.int32, (width, width), 0)
    lane = lax.broadcasted_iota(jnp.int32, (width, width), 1)
    identity = jnp.where(row == lane, 1.0, 0.0)
    inv_left = inverse_spd(identity + exact_dot(coupling, coupling, 1, 1))
    product = exact_dot(inv_left, coupling)
    lower_right = identity - 2.0 * exact_dot(coupling, product, 0, 0)
    top = jnp.concatenate([2.0 * inv_left - identity, 2.0 * product], axis=1)
    bottom = jnp.concatenate([-2.0 * product.T, lower_right], axis=1)
    return jnp.concatenate([top, bottom], axis=0)


def kernel(
    total_rows, col_count, matrix_ref, active_ref, out_ref,
    first, second, sending, result, relay, gram, norms, shared, arrived, rotor_parts,
    own_sem, a_send, a_recv, b_send, b_recv, g_send, g_recv, c_send, c_recv, local_sem,
):
    col, row = lax.axis_index("col"), lax.axis_index("row")
    odd = lax.rem(col, 2)
    pair = col // 2
    parity = lax.rem(pair, 2)
    half = lax.rem(odd + parity, 2)
    width = matrix_ref.shape[1]
    half_rows = matrix_ref.shape[0] // 2
    chunks = half_rows // CHUNK
    upper_col = 2 * pair

    def wrapped(position):
        return lax.rem(position + col_count, col_count)

    partner = (col + 1 - 2 * odd, row)
    sibling = (col, row + 1 - 2 * lax.rem(row, 2))
    beside = (col, lax.rem(row + 2, 4))
    b_target = (wrapped(upper_col + 3 - odd), row)
    b_source = (wrapped(upper_col - 1 - odd), row)

    barrier = pltpu.get_barrier_semaphore()
    for device in (partner, sibling, beside, b_target, b_source):
        pl.semaphore_signal(barrier, inc=1, device_id=device, device_id_type=MESH)
    pl.semaphore_wait(barrier, 5)

    def rows_of(which, chunk):
        return pl.ds(pl.multiple_of(which * half_rows + chunk * CHUNK, CHUNK), CHUNK)

    def a_copy(chunk):
        return pltpu.make_async_remote_copy(
            src_ref=matrix_ref.at[rows_of(1 - half, chunk)],
            dst_ref=first.at[odd, rows_of(0, chunk)],
            send_sem=a_send.at[chunk],
            recv_sem=a_recv.at[chunk],
            device_id=partner,
            device_id_type=MESH,
        )

    def b_copy(chunk):
        return pltpu.make_async_remote_copy(
            src_ref=sending.at[rows_of(0, chunk)],
            dst_ref=second.at[0, rows_of(0, chunk)],
            send_sem=b_send.at[chunk],
            recv_sem=b_recv.at[chunk],
            device_id=b_target,
            device_id_type=MESH,
        )

    def to_output(source, send, recv, chunk, device):
        return pltpu.make_async_remote_copy(
            src_ref=source.at[rows_of(0, chunk)],
            dst_ref=out_ref.at[rows_of(half, chunk)],
            send_sem=send.at[chunk],
            recv_sem=recv.at[chunk],
            device_id=device,
            device_id_type=MESH,
        )

    def c_upper(chunk):
        return to_output(result.at[0], c_send.at[0], c_recv.at[0], chunk, partner)

    def c_lower(chunk):
        return to_output(result.at[1], c_send.at[1], c_recv.at[1], chunk, b_target)

    def c_passed(chunk):
        return to_output(relay, c_send.at[0], c_recv.at[0], chunk, partner)

    def c_relay(chunk):
        return pltpu.make_async_remote_copy(
            src_ref=result.at[1, rows_of(0, chunk)],
            dst_ref=relay.at[rows_of(0, chunk)],
            send_sem=c_send.at[1, chunk],
            recv_sem=c_recv.at[1, chunk],
            device_id=b_target,
            device_id_type=MESH,
        )

    def c_local(chunk):
        return pltpu.make_async_copy(
            result.at[0, rows_of(0, chunk)], out_ref.at[rows_of(half, chunk)], local_sem.at[chunk]
        )

    def each_chunk(body):
        lax.fori_loop(0, chunks, lambda chunk, carry: (body(chunk), carry)[1], 0)

    own = pltpu.make_async_copy(
        matrix_ref.at[pl.ds(pl.multiple_of(half * half_rows, CHUNK), half_rows)], first.at[odd], own_sem
    )
    each_chunk(lambda chunk: a_copy(chunk).start())
    own.start()

    def clear():
        gram[...] = jnp.zeros_like(gram)
        norms[...] = jnp.zeros_like(norms)

    def add_gram(held, chunk):
        upper = held[0, rows_of(0, chunk)]
        lower = held[1, rows_of(0, chunk)]
        gram[...] += lax.dot_general(
            jnp.concatenate(split(upper), axis=1),
            jnp.concatenate(split(lower), axis=1),
            (((0,), (0,)), ((), ())),
            preferred_element_type=jnp.float32,
        )
        norms[0] += jnp.sum((upper * upper).reshape(CHUNK // 8, 8, width), axis=0)
        norms[1] += jnp.sum((lower * lower).reshape(CHUNK // 8, 8, width), axis=0)

    def make_rotor(step):
        shared[step, 0, :width] = (gram[:width, :width] + gram[width:, width:]) + (
            gram[:width, width:] + gram[width:, :width]
        )
        shared[step, 0, width : width + 8] = norms[0]
        shared[step, 0, width + 8 :] = norms[1]
        for stage, device in enumerate((sibling, beside, partner)):
            copy = pltpu.make_async_remote_copy(
                src_ref=shared.at[step, stage],
                dst_ref=arrived.at[step, stage],
                send_sem=g_send.at[step, stage],
                recv_sem=g_recv.at[step, stage],
                device_id=device,
                device_id_type=MESH,
            )
            copy.start()
            copy.wait()
            shared[step, stage + 1] = shared[step, stage] + arrived[step, stage]
        flag = active_ref[step, pair].astype(jnp.float32)
        high, low = split(rotor_of(shared[step, 3], flag, total_rows))
        rotor_parts[: 2 * width] = high
        rotor_parts[2 * width : 4 * width] = high
        rotor_parts[4 * width :] = low

    def turned(held, chunk):
        paired = jnp.concatenate([held[0, rows_of(0, chunk)], held[1, rows_of(0, chunk)]], axis=1)
        high, low = split(paired)
        return jnp.dot(
            jnp.concatenate([high, low, high], axis=1), rotor_parts[...], preferred_element_type=jnp.float32
        )

    clear()
    own.wait()

    def gather_first(chunk):
        a_copy(chunk).wait_recv()
        add_gram(first, chunk)

    each_chunk(gather_first)
    make_rotor(0)

    def turn_first(chunk):
        value = turned(first, chunk)
        sending[rows_of(0, chunk)] = value[:, width:]
        b_copy(chunk).start()
        second[1, rows_of(0, chunk)] = value[:, :width]

    each_chunk(turn_first)
    clear()

    def gather_second(chunk):
        b_copy(chunk).wait_recv()
        add_gram(second, chunk)

    each_chunk(gather_second)
    make_rotor(1)

    def turn_second(chunk):
        value = turned(second, chunk)
        result[1, rows_of(0, chunk)] = value[:, width:]
        result[0, rows_of(0, chunk)] = value[:, :width]

        @pl.when(odd == 0)
        def _():
            c_relay(chunk).start()
            c_upper(chunk).start()

        @pl.when(odd == 1)
        def _():
            c_lower(chunk).start()
            c_local(chunk).start()

    each_chunk(turn_second)

    @pl.when(odd == 1)
    def _():
        def pass_on(chunk):
            c_relay(chunk).wait_recv()
            c_passed(chunk).start()

        each_chunk(pass_on)

    def finish(chunk):
        a_copy(chunk).wait_send()
        b_copy(chunk).wait_send()
        c_lower(chunk).wait_send()
        c_upper(chunk).wait_send()
        c_upper(chunk).wait_recv()

        @pl.when(odd == 0)
        def _():
            c_lower(chunk).wait_recv()

        @pl.when(odd == 1)
        def _():
            c_local(chunk).wait()

    each_chunk(finish)


def solution(mesh):
    col_count = mesh.shape["col"]

    def on_device(matrix, active):
        rows, width = matrix.shape
        half_rows = rows // 2
        chunks = half_rows // CHUNK
        total_rows = rows * mesh.shape["row"]
        payload = width + 16
        dma = pltpu.SemaphoreType.DMA
        return pl.pallas_call(
            functools.partial(kernel, total_rows, col_count),
            out_shape=jax.ShapeDtypeStruct(matrix.shape, jnp.float32),
            in_specs=[pl.BlockSpec(memory_space=pl.ANY), pl.BlockSpec(memory_space=pltpu.SMEM)],
            out_specs=pl.BlockSpec(memory_space=pl.ANY),
            scratch_shapes=[
                pltpu.VMEM((2, half_rows, width), jnp.float32),
                pltpu.VMEM((2, half_rows, width), jnp.float32),
                pltpu.VMEM((half_rows, width), jnp.float32),
                pltpu.VMEM((2, half_rows, width), jnp.float32),
                pltpu.VMEM((half_rows, width), jnp.float32),
                pltpu.VMEM((2 * width, 2 * width), jnp.float32),
                pltpu.VMEM((2, 8, width), jnp.float32),
                pltpu.VMEM((2, 4, payload, width), jnp.float32),
                pltpu.VMEM((2, 3, payload, width), jnp.float32),
                pltpu.VMEM((6 * width, 2 * width), jnp.bfloat16),
                dma(()),
                dma((chunks,)),
                dma((chunks,)),
                dma((chunks,)),
                dma((chunks,)),
                dma((2, 3)),
                dma((2, 3)),
                dma((2, chunks)),
                dma((2, chunks)),
                dma((chunks,)),
            ],
            compiler_params=pltpu.CompilerParams(
                collective_id=0, has_side_effects=True, vmem_limit_bytes=40 * 2**20
            ),
            name="tournament",
        )(matrix, active)

    return jax.shard_map(
        on_device, mesh=mesh, in_specs=(P("row", "col"), P()), out_specs=P("row", "col"), check_vma=False
    )
```

```python
import functools
import math

import jax
import jax.numpy as jnp
from jax import lax
from jax.experimental import pallas as pl
from jax.experimental.pallas import tpu as pltpu
from jax.sharding import PartitionSpec as P

MESH = pl.DeviceIdType.MESH
CHUNK = 256
TILE = 8


def lane_spread(value, lane):
    return jnp.broadcast_to(value[:, lane : lane + 1], value.shape)


def eliminate(tiles, block):
    size = TILE
    first = size * block
    shape = tiles[0].shape
    lane = lax.broadcasted_iota(jnp.int32, shape, 1)
    row = lax.broadcasted_iota(jnp.int32, shape, 0)
    inside = (lane >= first) & (lane < first + size)
    rows = [jnp.broadcast_to(tiles[block][i : i + 1], shape) for i in range(size)]
    small = {(i, j): lane_spread(rows[i], first + j) for i in range(size) for j in range(i, size)}
    rows = [jnp.where(inside, jnp.where(lane == first + i, 1.0, 0.0), rows[i]) for i in range(size)]
    inverse, ratio = [None] * size, {}
    for i in range(size):
        if i % 2 == 0:
            head, side, tail = small[i, i], small[i, i + 1], small[i + 1, i + 1]
            inverse[i] = 1.0 / head
            inverse[i + 1] = head * (1.0 / (head * tail - side * side))
        for k in range(i + 1, size):
            ratio[i, k] = small[i, k] * inverse[i]
            for j in range(k, size):
                small[k, j] = small[k, j] - ratio[i, k] * small[i, j]
            rows[k] = rows[k] - ratio[i, k] * rows[i]
    for i in reversed(range(size)):
        rows[i] = rows[i] * inverse[i]
        for k in range(i + 1, size):
            rows[i] = rows[i] - ratio[i, k] * rows[k]
    result = list(tiles)
    for other in range(len(tiles)):
        if other != block:
            value = jnp.where(inside, 0.0, tiles[other])
            for i in range(size):
                value = value - lane_spread(tiles[other], first + i) * rows[i]
            result[other] = value
    solved = rows[0]
    for i in range(1, size):
        solved = jnp.where(row == i, rows[i], solved)
    result[block] = solved
    return result


def inverse_spd(matrix_in):
    order = matrix_in.shape[0]
    tiles = [matrix_in[i : i + TILE] for i in range(0, order, TILE)]
    for block in range(order // TILE):
        tiles = eliminate(tiles, block)
    return jnp.concatenate(tiles, axis=0)


def split(value):
    high = value.astype(jnp.bfloat16)
    return high, (value - high.astype(jnp.float32)).astype(jnp.bfloat16)


def exact_dot(left, right, left_dim=1, right_dim=0):
    return lax.dot_general(
        left,
        right,
        (((left_dim,), (right_dim,)), ((), ())),
        precision=lax.Precision.HIGHEST,
        preferred_element_type=jnp.float32,
    )


def rotor_of(cross, norm_upper, norm_lower, flag, total_rows):
    width = cross.shape[1]
    scale_upper = 1.0 / jnp.sqrt(jnp.sum(norm_upper, axis=0, keepdims=True) / total_rows + 1e-06)
    scale_lower = 1.0 / jnp.sqrt(jnp.sum(norm_lower, axis=0, keepdims=True) / total_rows + 1e-06)
    scale_rows = jnp.broadcast_to(scale_upper, (width, width)).T
    coupling = 0.25 / math.sqrt(total_rows * width) * flag * scale_rows * cross * scale_lower
    row = lax.broadcasted_iota(jnp.int32, (width, width), 0)
    lane = lax.broadcasted_iota(jnp.int32, (width, width), 1)
    identity = jnp.where(row == lane, 1.0, 0.0)
    inv_left = inverse_spd(identity + exact_dot(coupling, coupling, 1, 1))
    product = exact_dot(inv_left, coupling)
    lower_right = identity - 2.0 * exact_dot(coupling, product, 0, 0)
    top = jnp.concatenate([2.0 * inv_left - identity, 2.0 * product], axis=1)
    bottom = jnp.concatenate([-2.0 * product.T, lower_right], axis=1)
    return jnp.concatenate([top, bottom], axis=0)


def kernel(
    total_rows, col_count, matrix_ref, active_ref, out_ref,
    first, second, sending, result, relay, gram, norms, partial, arrived, summed, shared, rotor_parts, flags,
    flag_sem, own_sem, a_send, a_recv, b_send, b_recv, g_send, g_recv, c_send, c_recv, local_sem,
):
    col, row = lax.axis_index("col"), lax.axis_index("row")
    odd, core = lax.rem(col, 2), lax.rem(row, 2)
    pair = col // 2
    parity = lax.rem(pair, 2)
    half = lax.rem(odd + parity, 2)
    width = matrix_ref.shape[1]
    half_rows = matrix_ref.shape[0] // 2
    chunks = half_rows // CHUNK
    upper_col = 2 * pair

    def wrapped(position):
        return lax.rem(position + col_count, col_count)

    partner = (col + 1 - 2 * odd, row)
    sibling = (col, row + 1 - 2 * lax.rem(row, 2))
    beside = (col, lax.rem(row + 2, 4))
    across = (col + 1 - 2 * odd, lax.rem(row + 2, 4))
    b_target = (wrapped(upper_col + 3 - odd), row)
    b_source = (wrapped(upper_col - 1 - odd), row)

    barrier = pltpu.get_barrier_semaphore()
    for device in (partner, sibling, beside, across, b_target, b_source):
        pl.semaphore_signal(barrier, inc=1, device_id=device, device_id_type=MESH)
    pl.semaphore_wait(barrier, 6)

    def rows_of(which, chunk):
        return pl.ds(pl.multiple_of(which * half_rows + chunk * CHUNK, CHUNK), CHUNK)

    def a_copy(chunk):
        return pltpu.make_async_remote_copy(
            src_ref=matrix_ref.at[rows_of(1 - half, chunk)],
            dst_ref=first.at[odd, rows_of(0, chunk)],
            send_sem=a_send.at[chunk],
            recv_sem=a_recv.at[chunk],
            device_id=partner,
            device_id_type=MESH,
        )

    def b_copy(chunk):
        return pltpu.make_async_remote_copy(
            src_ref=sending.at[rows_of(0, chunk)],
            dst_ref=second.at[0, rows_of(0, chunk)],
            send_sem=b_send.at[chunk],
            recv_sem=b_recv.at[chunk],
            device_id=b_target,
            device_id_type=MESH,
        )

    def to_output(source, send, recv, chunk, device):
        return pltpu.make_async_remote_copy(
            src_ref=source.at[rows_of(0, chunk)],
            dst_ref=out_ref.at[rows_of(half, chunk)],
            send_sem=send.at[chunk],
            recv_sem=recv.at[chunk],
            device_id=device,
            device_id_type=MESH,
        )

    def c_upper(chunk):
        return to_output(result.at[0], c_send.at[0], c_recv.at[0], chunk, partner)

    def c_lower(chunk):
        return to_output(result.at[1], c_send.at[1], c_recv.at[1], chunk, b_target)

    def c_passed(chunk):
        return to_output(relay, c_send.at[0], c_recv.at[0], chunk, partner)

    def c_relay(chunk):
        return pltpu.make_async_remote_copy(
            src_ref=result.at[1, rows_of(0, chunk)],
            dst_ref=relay.at[rows_of(0, chunk)],
            send_sem=c_send.at[1, chunk],
            recv_sem=c_recv.at[1, chunk],
            device_id=b_target,
            device_id_type=MESH,
        )

    def c_local(chunk):
        return pltpu.make_async_copy(
            result.at[0, rows_of(0, chunk)], out_ref.at[rows_of(half, chunk)], local_sem.at[chunk]
        )

    def g_copy(source, target, step, stage, device):
        return pltpu.make_async_remote_copy(
            src_ref=source,
            dst_ref=target,
            send_sem=g_send.at[step, stage],
            recv_sem=g_recv.at[step, stage],
            device_id=device,
            device_id_type=MESH,
        )

    def each_chunk(body):
        lax.fori_loop(0, chunks, lambda chunk, carry: (body(chunk), carry)[1], 0)

    own = pltpu.make_async_copy(
        matrix_ref.at[pl.ds(pl.multiple_of(half * half_rows, CHUNK), half_rows)], first.at[odd], own_sem
    )
    each_chunk(lambda chunk: a_copy(chunk).start())
    own.start()
    flag_copy = pltpu.make_async_copy(active_ref, flags, flag_sem)
    flag_copy.start()

    def clear():
        gram[...] = jnp.zeros_like(gram)
        norms[...] = jnp.zeros_like(norms)

    def add_gram(held, chunk):
        upper = held[0, rows_of(0, chunk)]
        lower = held[1, rows_of(0, chunk)]
        gram[...] += lax.dot_general(
            jnp.concatenate(split(upper), axis=1),
            jnp.concatenate(split(lower), axis=1),
            (((0,), (0,)), ((), ())),
            preferred_element_type=jnp.float32,
        )
        norms[0] += jnp.sum((upper * upper).reshape(CHUNK // 8, 8, width), axis=0)
        norms[1] += jnp.sum((lower * lower).reshape(CHUNK // 8, 8, width), axis=0)

    def make_rotor(step):
        middle = width // 2
        cross = (gram[:width, :width] + gram[width:, width:]) + (gram[:width, width:] + gram[width:, :width])
        for part in range(2):
            partial[step, part, :middle] = cross[part * middle : (part + 1) * middle]
            partial[step, part, middle:] = norms[part]
        copy = g_copy(partial.at[step, 1 - core], arrived.at[step, 0], step, 0, sibling)
        copy.start()
        copy.wait()
        summed[step] = partial[step, core] + arrived[step, 0]
        copies = [
            g_copy(summed.at[step], arrived.at[step, stage], step, stage, device)
            for stage, device in ((1, partner), (2, beside), (3, across))
        ]
        for copy in copies:
            copy.start()
        for copy in copies:
            copy.wait()
        shared[step, core] = (summed[step] + arrived[step, 1]) + (arrived[step, 2] + arrived[step, 3])
        copy = g_copy(shared.at[step, core], shared.at[step, core], step, 4, sibling)
        copy.start()
        copy.wait()
        flag = flags[step, pair].astype(jnp.float32)
        cross = jnp.concatenate([shared[step, 0, :middle], shared[step, 1, :middle]], axis=0)
        rotor = rotor_of(cross, shared[step, 0, middle:], shared[step, 1, middle:], flag, total_rows)
        high, low = split(rotor)
        rotor_parts[: 2 * width] = high
        rotor_parts[2 * width : 4 * width] = high
        rotor_parts[4 * width :] = low

    def turned(held, chunk):
        paired = jnp.concatenate([held[0, rows_of(0, chunk)], held[1, rows_of(0, chunk)]], axis=1)
        high, low = split(paired)
        return jnp.dot(
            jnp.concatenate([high, low, high], axis=1), rotor_parts[...], preferred_element_type=jnp.float32
        )

    clear()
    own.wait()
    flag_copy.wait()

    def gather_first(chunk):
        a_copy(chunk).wait_recv()
        add_gram(first, chunk)

    each_chunk(gather_first)
    make_rotor(0)

    def turn_first(chunk):
        value = turned(first, chunk)
        sending[rows_of(0, chunk)] = value[:, width:]
        b_copy(chunk).start()
        second[1, rows_of(0, chunk)] = value[:, :width]

    each_chunk(turn_first)
    clear()

    def gather_second(chunk):
        b_copy(chunk).wait_recv()
        add_gram(second, chunk)

    each_chunk(gather_second)
    make_rotor(1)

    def turn_second(chunk):
        value = turned(second, chunk)
        result[1, rows_of(0, chunk)] = value[:, width:]
        result[0, rows_of(0, chunk)] = value[:, :width]

        @pl.when(odd == 0)
        def _():
            c_relay(chunk).start()
            c_upper(chunk).start()

        @pl.when(odd == 1)
        def _():
            c_lower(chunk).start()
            c_local(chunk).start()

    each_chunk(turn_second)

    @pl.when(odd == 1)
    def _():
        def pass_on(chunk):
            c_relay(chunk).wait_recv()
            c_passed(chunk).start()

        each_chunk(pass_on)

    def finish(chunk):
        a_copy(chunk).wait_send()
        b_copy(chunk).wait_send()
        c_lower(chunk).wait_send()
        c_upper(chunk).wait_send()
        c_upper(chunk).wait_recv()

        @pl.when(odd == 0)
        def _():
            c_lower(chunk).wait_recv()

        @pl.when(odd == 1)
        def _():
            c_local(chunk).wait()

    each_chunk(finish)


def solution(mesh):
    col_count = mesh.shape["col"]

    def on_device(matrix, active):
        rows, width = matrix.shape
        half_rows = rows // 2
        chunks = half_rows // CHUNK
        total_rows = rows * mesh.shape["row"]
        payload = width // 2 + TILE
        dma = pltpu.SemaphoreType.DMA
        return pl.pallas_call(
            functools.partial(kernel, total_rows, col_count),
            out_shape=jax.ShapeDtypeStruct(matrix.shape, jnp.float32),
            in_specs=[pl.BlockSpec(memory_space=pl.ANY)] * 2,
            out_specs=pl.BlockSpec(memory_space=pl.ANY),
            scratch_shapes=[
                pltpu.VMEM((2, half_rows, width), jnp.float32),
                pltpu.VMEM((2, half_rows, width), jnp.float32),
                pltpu.VMEM((half_rows, width), jnp.float32),
                pltpu.VMEM((2, half_rows, width), jnp.float32),
                pltpu.VMEM((half_rows, width), jnp.float32),
                pltpu.VMEM((2 * width, 2 * width), jnp.float32),
                pltpu.VMEM((2, 8, width), jnp.float32),
                pltpu.VMEM((2, 2, payload, width), jnp.float32),
                pltpu.VMEM((2, 4, payload, width), jnp.float32),
                pltpu.VMEM((2, payload, width), jnp.float32),
                pltpu.VMEM((2, 2, payload, width), jnp.float32),
                pltpu.VMEM((6 * width, 2 * width), jnp.bfloat16),
                pltpu.SMEM(active.shape, jnp.int32),
                dma(()),
                dma(()),
                dma((chunks,)),
                dma((chunks,)),
                dma((chunks,)),
                dma((chunks,)),
                dma((2, 5)),
                dma((2, 5)),
                dma((2, chunks)),
                dma((2, chunks)),
                dma((chunks,)),
            ],
            compiler_params=pltpu.CompilerParams(
                collective_id=0, has_side_effects=True, vmem_limit_bytes=50 * 2**20
            ),
            name="tournament",
        )(matrix, active)

    return jax.shard_map(
        on_device, mesh=mesh, in_specs=(P("row", "col"), P()), out_specs=P("row", "col"), check_vma=False
    )
```

```python
import functools
import math

import jax
import jax.numpy as jnp
from jax import lax
from jax.experimental import pallas as pl
from jax.experimental.pallas import tpu as pltpu
from jax.sharding import PartitionSpec as P

MESH = pl.DeviceIdType.MESH
CHUNK = 256
TILE = 8
AHEAD = 4


def lane_spread(value, lane):
    return jnp.broadcast_to(value[:, lane : lane + 1], value.shape)


def eliminate(tiles, block):
    size = TILE
    first = size * block
    shape = tiles[0].shape
    lane = lax.broadcasted_iota(jnp.int32, shape, 1)
    row = lax.broadcasted_iota(jnp.int32, shape, 0)
    inside = (lane >= first) & (lane < first + size)
    rows = [jnp.broadcast_to(tiles[block][i : i + 1], shape) for i in range(size)]
    small = {(i, j): lane_spread(rows[i], first + j) for i in range(size) for j in range(i, size)}
    rows = [jnp.where(inside, jnp.where(lane == first + i, 1.0, 0.0), rows[i]) for i in range(size)]
    inverse, ratio = [None] * size, {}
    for i in range(size):
        if i % 2 == 0:
            head, side, tail = small[i, i], small[i, i + 1], small[i + 1, i + 1]
            inverse[i] = 1.0 / head
            inverse[i + 1] = head * (1.0 / (head * tail - side * side))
        for k in range(i + 1, size):
            ratio[i, k] = small[i, k] * inverse[i]
            for j in range(k, size):
                small[k, j] = small[k, j] - ratio[i, k] * small[i, j]
            rows[k] = rows[k] - ratio[i, k] * rows[i]
    for i in reversed(range(size)):
        rows[i] = rows[i] * inverse[i]
        for k in range(i + 1, size):
            rows[i] = rows[i] - ratio[i, k] * rows[k]
    result = list(tiles)
    for other in range(len(tiles)):
        if other != block:
            value = jnp.where(inside, 0.0, tiles[other])
            for i in range(size):
                value = value - lane_spread(tiles[other], first + i) * rows[i]
            result[other] = value
    solved = rows[0]
    for i in range(1, size):
        solved = jnp.where(row == i, rows[i], solved)
    result[block] = solved
    return result


def inverse_spd(matrix_in):
    order = matrix_in.shape[0]
    tiles = [matrix_in[i : i + TILE] for i in range(0, order, TILE)]
    for block in range(order // TILE):
        tiles = eliminate(tiles, block)
    return jnp.concatenate(tiles, axis=0)


def split(value):
    high = value.astype(jnp.bfloat16)
    return high, (value - high.astype(jnp.float32)).astype(jnp.bfloat16)


def exact_dot(left, right, left_dim=1, right_dim=0):
    return lax.dot_general(
        left,
        right,
        (((left_dim,), (right_dim,)), ((), ())),
        precision=lax.Precision.HIGHEST,
        preferred_element_type=jnp.float32,
    )


def rotor_of(cross, norm_upper, norm_lower, flag, total_rows):
    width = cross.shape[1]
    scale_upper = 1.0 / jnp.sqrt(jnp.sum(norm_upper, axis=0, keepdims=True) / total_rows + 1e-06)
    scale_lower = 1.0 / jnp.sqrt(jnp.sum(norm_lower, axis=0, keepdims=True) / total_rows + 1e-06)
    scale_rows = jnp.broadcast_to(scale_upper, (width, width)).T
    coupling = 0.25 / math.sqrt(total_rows * width) * flag * scale_rows * cross * scale_lower
    row = lax.broadcasted_iota(jnp.int32, (width, width), 0)
    lane = lax.broadcasted_iota(jnp.int32, (width, width), 1)
    identity = jnp.where(row == lane, 1.0, 0.0)
    inv_left = inverse_spd(identity + exact_dot(coupling, coupling, 1, 1))
    product = exact_dot(inv_left, coupling)
    lower_right = identity - 2.0 * exact_dot(coupling, product, 0, 0)
    top = jnp.concatenate([2.0 * inv_left - identity, 2.0 * product], axis=1)
    bottom = jnp.concatenate([-2.0 * product.T, lower_right], axis=1)
    return jnp.concatenate([top, bottom], axis=0)


def kernel(
    total_rows, col_count, matrix_ref, active_ref, out_ref,
    first, raw, second, sending, result, relay, gram, norms, partial, arrived, summed, shared, rotor_parts, raw_parts, rotor_out, rotor_in, flags,
    flag_sem, own_sem, a_send, a_recv, r_send, r_recv, h_send, h_recv, b_send, b_recv, g_send, g_recv, c_send, c_recv, local_sem,
):
    col, row = lax.axis_index("col"), lax.axis_index("row")
    odd, core = lax.rem(col, 2), lax.rem(row, 2)
    pair = col // 2
    parity = lax.rem(pair, 2)
    half = lax.rem(odd + parity, 2)
    width = matrix_ref.shape[1]
    half_rows = matrix_ref.shape[0] // 2
    chunks = half_rows // CHUNK
    upper_col = 2 * pair

    def wrapped(position):
        return lax.rem(position + col_count, col_count)

    partner = (col + 1 - 2 * odd, row)
    sibling = (col, row + 1 - 2 * lax.rem(row, 2))
    beside = (col, lax.rem(row + 2, 4))
    across = (col + 1 - 2 * odd, lax.rem(row + 2, 4))
    b_target = (wrapped(upper_col + 3 - odd), row)
    b_source = (wrapped(upper_col - 1 - odd), row)

    barrier = pltpu.get_barrier_semaphore()
    for device in (partner, sibling, beside, across, b_target, b_source):
        pl.semaphore_signal(barrier, inc=1, device_id=device, device_id_type=MESH)
    pl.semaphore_wait(barrier, 6)

    def rows_of(which, chunk):
        return pl.ds(pl.multiple_of(which * half_rows + chunk * CHUNK, CHUNK), CHUNK)

    def a_copy(chunk):
        return pltpu.make_async_remote_copy(
            src_ref=matrix_ref.at[rows_of(1 - half, chunk)],
            dst_ref=first.at[odd, rows_of(0, chunk)],
            send_sem=a_send.at[chunk],
            recv_sem=a_recv.at[chunk],
            device_id=partner,
            device_id_type=MESH,
        )

    def r_copy(side, chunk):
        source = (matrix_ref.at[rows_of(half, chunk)], first.at[1 - odd, rows_of(0, chunk)])[side]
        return pltpu.make_async_remote_copy(
            src_ref=source,
            dst_ref=raw.at[(odd, 1 - odd)[side], rows_of(0, chunk)],
            send_sem=r_send.at[side, chunk],
            recv_sem=r_recv.at[side, chunk],
            device_id=b_target,
            device_id_type=MESH,
        )

    def h_copy():
        return pltpu.make_async_remote_copy(
            src_ref=rotor_out,
            dst_ref=rotor_in,
            send_sem=h_send,
            recv_sem=h_recv,
            device_id=b_target,
            device_id_type=MESH,
        )

    def b_copy(chunk):
        return pltpu.make_async_remote_copy(
            src_ref=sending.at[rows_of(0, chunk)],
            dst_ref=second.at[0, rows_of(0, chunk)],
            send_sem=b_send.at[chunk],
            recv_sem=b_recv.at[chunk],
            device_id=b_target,
            device_id_type=MESH,
        )

    def to_output(source, send, recv, chunk, device):
        return pltpu.make_async_remote_copy(
            src_ref=source.at[rows_of(0, chunk)],
            dst_ref=out_ref.at[rows_of(half, chunk)],
            send_sem=send.at[chunk],
            recv_sem=recv.at[chunk],
            device_id=device,
            device_id_type=MESH,
        )

    def c_upper(chunk):
        return to_output(result.at[0], c_send.at[0], c_recv.at[0], chunk, partner)

    def c_lower(chunk):
        return to_output(result.at[1], c_send.at[1], c_recv.at[1], chunk, b_target)

    def c_passed(chunk):
        return to_output(relay, c_send.at[0], c_recv.at[0], chunk, partner)

    def c_relay(chunk):
        return pltpu.make_async_remote_copy(
            src_ref=result.at[1, rows_of(0, chunk)],
            dst_ref=relay.at[rows_of(0, chunk)],
            send_sem=c_send.at[1, chunk],
            recv_sem=c_recv.at[1, chunk],
            device_id=b_target,
            device_id_type=MESH,
        )

    def c_local(chunk):
        return pltpu.make_async_copy(
            result.at[0, rows_of(0, chunk)], out_ref.at[rows_of(half, chunk)], local_sem.at[chunk]
        )

    def g_copy(source, target, step, stage, device):
        return pltpu.make_async_remote_copy(
            src_ref=source,
            dst_ref=target,
            send_sem=g_send.at[step, stage],
            recv_sem=g_recv.at[step, stage],
            device_id=device,
            device_id_type=MESH,
        )

    def each_chunk(body, low=0, high=chunks):
        lax.fori_loop(low, high, lambda chunk, carry: (body(chunk), carry)[1], 0)

    own = pltpu.make_async_copy(
        matrix_ref.at[pl.ds(pl.multiple_of(half * half_rows, CHUNK), half_rows)], first.at[odd], own_sem
    )
    each_chunk(lambda chunk: (a_copy(chunk).start(), r_copy(0, chunk).start()), 0, AHEAD)
    each_chunk(lambda chunk: a_copy(chunk).start(), AHEAD)
    own.start()
    flag_copy = pltpu.make_async_copy(active_ref, flags, flag_sem)
    flag_copy.start()

    def clear():
        gram[...] = jnp.zeros_like(gram)
        norms[...] = jnp.zeros_like(norms)

    def add_gram(held, chunk):
        upper = held[0, rows_of(0, chunk)]
        lower = held[1, rows_of(0, chunk)]
        gram[...] += lax.dot_general(
            jnp.concatenate(split(upper), axis=1),
            jnp.concatenate(split(lower), axis=1),
            (((0,), (0,)), ((), ())),
            preferred_element_type=jnp.float32,
        )
        norms[0] += jnp.sum((upper * upper).reshape(CHUNK // 8, 8, width), axis=0)
        norms[1] += jnp.sum((lower * lower).reshape(CHUNK // 8, 8, width), axis=0)

    def make_rotor(step):
        middle = width // 2
        cross = (gram[:width, :width] + gram[width:, width:]) + (gram[:width, width:] + gram[width:, :width])
        for part in range(2):
            partial[step, part, :middle] = cross[part * middle : (part + 1) * middle]
            partial[step, part, middle:] = norms[part]
        copy = g_copy(partial.at[step, 1 - core], arrived.at[step, 0], step, 0, sibling)
        copy.start()
        copy.wait()
        summed[step] = partial[step, core] + arrived[step, 0]
        copies = [
            g_copy(summed.at[step], arrived.at[step, stage], step, stage, device)
            for stage, device in ((1, partner), (2, beside), (3, across))
        ]
        for copy in copies:
            copy.start()
        for copy in copies:
            copy.wait()
        shared[step, core] = (summed[step] + arrived[step, 1]) + (arrived[step, 2] + arrived[step, 3])
        copy = g_copy(shared.at[step, core], shared.at[step, core], step, 4, sibling)
        copy.start()
        copy.wait()
        flag = flags[step, pair].astype(jnp.float32)
        cross = jnp.concatenate([shared[step, 0, :middle], shared[step, 1, :middle]], axis=0)
        rotor = rotor_of(cross, shared[step, 0, middle:], shared[step, 1, middle:], flag, total_rows)
        return rotor

    def stack(parts, value):
        high, low = split(value)
        parts[: 2 * width] = high
        parts[2 * width : 4 * width] = high
        parts[4 * width :] = low

    def paired(held, chunk):
        high, low = split(jnp.concatenate([held[0, rows_of(0, chunk)], held[1, rows_of(0, chunk)]], axis=1))
        return jnp.concatenate([high, low, high], axis=1)

    def turned(held, chunk, parts):
        return jnp.dot(paired(held, chunk), parts, preferred_element_type=jnp.float32)

    clear()
    own.wait()
    flag_copy.wait()

    def gather_first(chunk):
        a_copy(chunk).wait_recv()
        add_gram(first, chunk)

    def gather_and_pass(chunk):
        a_copy(chunk).wait_recv()
        r_copy(1, chunk).start()
        add_gram(first, chunk)

    each_chunk(gather_and_pass, 0, AHEAD)
    each_chunk(gather_first, AHEAD)
    rotor = make_rotor(0)
    rotor_out[...] = rotor[:, width:]
    h_copy().start()
    stack(rotor_parts, rotor)

    def turn_first(chunk):
        value = turned(first, chunk, rotor_parts[...])
        sending[rows_of(0, chunk)] = value[:, width:]
        b_copy(chunk).start()
        second[1, rows_of(0, chunk)] = value[:, :width]

    def turn_upper(chunk):
        second[1, rows_of(0, chunk)] = turned(first, chunk, rotor_parts[:, :width])

    each_chunk(turn_first, AHEAD)
    each_chunk(turn_upper, 0, AHEAD)
    clear()
    h_copy().wait_recv()
    stack(raw_parts, rotor_in[...])

    def turn_raw(chunk):
        r_copy(0, chunk).wait_recv()
        r_copy(1, chunk).wait_recv()
        second[0, rows_of(0, chunk)] = turned(raw, chunk, raw_parts[...])
        add_gram(second, chunk)

    def gather_second(chunk):
        b_copy(chunk).wait_recv()
        add_gram(second, chunk)

    each_chunk(turn_raw, 0, AHEAD)
    each_chunk(gather_second, AHEAD)
    stack(rotor_parts, make_rotor(1))

    def turn_second(chunk):
        value = turned(second, chunk, rotor_parts[...])
        result[1, rows_of(0, chunk)] = value[:, width:]
        result[0, rows_of(0, chunk)] = value[:, :width]

        @pl.when(odd == 0)
        def _():
            c_relay(chunk).start()
            c_upper(chunk).start()

        @pl.when(odd == 1)
        def _():
            c_lower(chunk).start()
            c_local(chunk).start()

    each_chunk(turn_second)

    @pl.when(odd == 1)
    def _():
        def pass_on(chunk):
            c_relay(chunk).wait_recv()
            c_passed(chunk).start()

        each_chunk(pass_on)

    def finish(chunk):
        a_copy(chunk).wait_send()
        c_lower(chunk).wait_send()
        c_upper(chunk).wait_send()
        c_upper(chunk).wait_recv()

        @pl.when(odd == 0)
        def _():
            c_lower(chunk).wait_recv()

        @pl.when(odd == 1)
        def _():
            c_local(chunk).wait()

    each_chunk(finish)
    each_chunk(lambda chunk: (r_copy(0, chunk).wait_send(), r_copy(1, chunk).wait_send()), 0, AHEAD)
    each_chunk(lambda chunk: b_copy(chunk).wait_send(), AHEAD)
    h_copy().wait_send()


def solution(mesh):
    col_count = mesh.shape["col"]

    def on_device(matrix, active):
        rows, width = matrix.shape
        half_rows = rows // 2
        chunks = half_rows // CHUNK
        total_rows = rows * mesh.shape["row"]
        payload = width // 2 + TILE
        dma = pltpu.SemaphoreType.DMA
        return pl.pallas_call(
            functools.partial(kernel, total_rows, col_count),
            out_shape=jax.ShapeDtypeStruct(matrix.shape, jnp.float32),
            in_specs=[pl.BlockSpec(memory_space=pl.ANY)] * 2,
            out_specs=pl.BlockSpec(memory_space=pl.ANY),
            scratch_shapes=[
                pltpu.VMEM((2, half_rows, width), jnp.float32),
                pltpu.VMEM((2, AHEAD * CHUNK, width), jnp.float32),
                pltpu.VMEM((2, half_rows, width), jnp.float32),
                pltpu.VMEM((half_rows, width), jnp.float32),
                pltpu.VMEM((2, half_rows, width), jnp.float32),
                pltpu.VMEM((half_rows, width), jnp.float32),
                pltpu.VMEM((2 * width, 2 * width), jnp.float32),
                pltpu.VMEM((2, 8, width), jnp.float32),
                pltpu.VMEM((2, 2, payload, width), jnp.float32),
                pltpu.VMEM((2, 4, payload, width), jnp.float32),
                pltpu.VMEM((2, payload, width), jnp.float32),
                pltpu.VMEM((2, 2, payload, width), jnp.float32),
                pltpu.VMEM((6 * width, 2 * width), jnp.bfloat16),
                pltpu.VMEM((6 * width, width), jnp.bfloat16),
                pltpu.VMEM((2 * width, width), jnp.float32),
                pltpu.VMEM((2 * width, width), jnp.float32),
                pltpu.SMEM(active.shape, jnp.int32),
                dma(()),
                dma(()),
                dma((chunks,)),
                dma((chunks,)),
                dma((2, AHEAD)),
                dma((2, AHEAD)),
                dma(()),
                dma(()),
                dma((chunks,)),
                dma((chunks,)),
                dma((2, 5)),
                dma((2, 5)),
                dma((2, chunks)),
                dma((2, chunks)),
                dma((chunks,)),
            ],
            compiler_params=pltpu.CompilerParams(
                collective_id=0, has_side_effects=True, vmem_limit_bytes=50 * 2**20
            ),
            name="tournament",
        )(matrix, active)

    return jax.shard_map(
        on_device, mesh=mesh, in_specs=(P("row", "col"), P()), out_specs=P("row", "col"), check_vma=False
    )
```

```python
import functools
import math

import jax
import jax.numpy as jnp
from jax import lax
from jax.experimental import pallas as pl
from jax.experimental.pallas import tpu as pltpu
from jax.sharding import PartitionSpec as P

MESH = pl.DeviceIdType.MESH
CHUNK = 256
TILE = 8
AHEAD = 6
SHORT = 5
PIECE = 256
WINDOW = 3
FLIGHT = 4


def lane_spread(value, lane):
    return jnp.broadcast_to(value[:, lane : lane + 1], value.shape)


def eliminate(tiles, block):
    size = TILE
    first = size * block
    shape = tiles[0].shape
    lane = lax.broadcasted_iota(jnp.int32, shape, 1)
    row = lax.broadcasted_iota(jnp.int32, shape, 0)
    inside = (lane >= first) & (lane < first + size)
    rows = [jnp.broadcast_to(tiles[block][i : i + 1], shape) for i in range(size)]
    small = {(i, j): lane_spread(rows[i], first + j) for i in range(size) for j in range(i, size)}
    rows = [jnp.where(inside, jnp.where(lane == first + i, 1.0, 0.0), rows[i]) for i in range(size)]
    inverse, ratio = [None] * size, {}
    for i in range(size):
        if i % 2 == 0:
            head, side, tail = small[i, i], small[i, i + 1], small[i + 1, i + 1]
            inverse[i] = 1.0 / head
            inverse[i + 1] = head * (1.0 / (head * tail - side * side))
        for k in range(i + 1, size):
            ratio[i, k] = small[i, k] * inverse[i]
            for j in range(k, size):
                small[k, j] = small[k, j] - ratio[i, k] * small[i, j]
            rows[k] = rows[k] - ratio[i, k] * rows[i]
    for i in reversed(range(size)):
        rows[i] = rows[i] * inverse[i]
        for k in range(i + 1, size):
            rows[i] = rows[i] - ratio[i, k] * rows[k]
    result = list(tiles)
    for other in range(len(tiles)):
        if other != block:
            value = jnp.where(inside, 0.0, tiles[other])
            spread = [lane_spread(tiles[other], first + i) for i in range(size)]
            upper = value - spread[7] * rows[7] - spread[6] * rows[6]
            lower = spread[5] * rows[5] + spread[4] * rows[4]
            early = spread[3] * rows[3] + spread[2] * rows[2]
            late = spread[1] * rows[1] + spread[0] * rows[0]
            result[other] = (upper - lower) - (early + late)
    solved = rows[0]
    for i in range(1, size):
        solved = jnp.where(row == i, rows[i], solved)
    result[block] = solved
    return result


def inverse_spd(matrix_in):
    order = matrix_in.shape[0]
    tiles = [matrix_in[i : i + TILE] for i in range(0, order, TILE)]
    for block in range(order // TILE):
        tiles = eliminate(tiles, block)
    return jnp.concatenate(tiles, axis=0)


def split(value):
    high = value.astype(jnp.bfloat16)
    return high, (value - high.astype(jnp.float32)).astype(jnp.bfloat16)


def exact_dot(left, right, left_dim=1, right_dim=0):
    return lax.dot_general(
        left,
        right,
        (((left_dim,), (right_dim,)), ((), ())),
        precision=lax.Precision.HIGHEST,
        preferred_element_type=jnp.float32,
    )


def rotor_of(cross, norm_upper, norm_lower, flag, total_rows):
    width = cross.shape[1]
    scale_upper = 1.0 / jnp.sqrt(jnp.sum(norm_upper, axis=0, keepdims=True) / total_rows + 1e-06)
    scale_lower = 1.0 / jnp.sqrt(jnp.sum(norm_lower, axis=0, keepdims=True) / total_rows + 1e-06)
    scale_rows = jnp.broadcast_to(scale_upper, (width, width)).T
    coupling = 0.25 / math.sqrt(total_rows * width) * flag * scale_rows * cross * scale_lower
    row = lax.broadcasted_iota(jnp.int32, (width, width), 0)
    lane = lax.broadcasted_iota(jnp.int32, (width, width), 1)
    identity = jnp.where(row == lane, 1.0, 0.0)
    inv_left = inverse_spd(identity + exact_dot(coupling, coupling, 1, 1))
    product = exact_dot(inv_left, coupling)
    lower_right = identity - 2.0 * exact_dot(coupling, product, 0, 0)
    top = jnp.concatenate([2.0 * inv_left - identity, 2.0 * product], axis=1)
    bottom = jnp.concatenate([-2.0 * product.T, lower_right], axis=1)
    return jnp.concatenate([top, bottom], axis=0)


def kernel(
    total_rows, col_count, matrix_ref, active_ref, out_ref,
    first, raw, second, sending, result, relay, gram, norms, partial, arrived, summed, shared, rotor_parts, raw_parts, rotor_out, rotor_in, flags,
    flag_sem, own_sem, a_send, a_recv, r_send, r_recv, h_send, h_recv, b_send, b_recv, g_send, g_recv, c_send, c_recv, local_sem,
):
    col, row = lax.axis_index("col"), lax.axis_index("row")
    odd, core = lax.rem(col, 2), lax.rem(row, 2)
    pair = col // 2
    parity = lax.rem(pair, 2)
    half = lax.rem(odd + parity, 2)
    width = matrix_ref.shape[1]
    half_rows = matrix_ref.shape[0] // 2
    chunks = half_rows // CHUNK
    upper_col = 2 * pair

    def wrapped(position):
        return lax.rem(position + col_count, col_count)

    partner = (col + 1 - 2 * odd, row)
    sibling = (col, row + 1 - 2 * lax.rem(row, 2))
    beside = (col, lax.rem(row + 2, 4))
    across = (col + 1 - 2 * odd, lax.rem(row + 2, 4))
    b_target = (wrapped(upper_col + 3 - odd), row)
    b_source = (wrapped(upper_col - 1 - odd), row)

    barrier = pltpu.get_barrier_semaphore()
    for device in (partner, sibling, beside, across, b_target, b_source):
        pl.semaphore_signal(barrier, inc=1, device_id=device, device_id_type=MESH)
    pl.semaphore_wait(barrier, 6)

    ahead_out = AHEAD - (AHEAD - SHORT) * parity
    ahead_in = SHORT + (AHEAD - SHORT) * parity

    def rows_of(which, chunk):
        return pl.ds(pl.multiple_of(which * half_rows + chunk * CHUNK, CHUNK), CHUNK)

    def a_copy(chunk):
        return pltpu.make_async_remote_copy(
            src_ref=matrix_ref.at[rows_of(1 - half, chunk)],
            dst_ref=first.at[odd, rows_of(0, chunk)],
            send_sem=a_send.at[chunk],
            recv_sem=a_recv.at[chunk],
            device_id=partner,
            device_id_type=MESH,
        )

    def r_copy(side, chunk):
        source = (matrix_ref.at[rows_of(half, chunk)], first.at[1 - odd, rows_of(0, chunk)])[side]
        return pltpu.make_async_remote_copy(
            src_ref=source,
            dst_ref=raw.at[(odd, 1 - odd)[side], rows_of(0, chunk)],
            send_sem=r_send.at[side, chunk],
            recv_sem=r_recv.at[side, chunk],
            device_id=b_target,
            device_id_type=MESH,
        )

    def h_copy():
        return pltpu.make_async_remote_copy(
            src_ref=rotor_out,
            dst_ref=rotor_in,
            send_sem=h_send,
            recv_sem=h_recv,
            device_id=b_target,
            device_id_type=MESH,
        )

    def b_copy(chunk):
        return pltpu.make_async_remote_copy(
            src_ref=sending.at[rows_of(0, chunk)],
            dst_ref=second.at[0, rows_of(0, chunk)],
            send_sem=b_send.at[chunk],
            recv_sem=b_recv.at[chunk],
            device_id=b_target,
            device_id_type=MESH,
        )

    def piece_of(which, piece):
        return pl.ds(pl.multiple_of(which * half_rows + piece * PIECE, PIECE), PIECE)

    def to_output(source, send, recv, piece, device):
        return pltpu.make_async_remote_copy(
            src_ref=source.at[piece_of(0, piece)],
            dst_ref=out_ref.at[piece_of(half, piece)],
            send_sem=send.at[piece],
            recv_sem=recv.at[piece],
            device_id=device,
            device_id_type=MESH,
        )

    def c_upper(piece):
        return to_output(result.at[0], c_send.at[0], c_recv.at[0], piece, partner)

    def c_lower(piece):
        return to_output(result.at[1], c_send.at[1], c_recv.at[1], piece, b_target)

    def c_passed(piece):
        return to_output(relay, c_send.at[0], c_recv.at[0], piece, partner)

    def c_relay(piece):
        return pltpu.make_async_remote_copy(
            src_ref=result.at[1, piece_of(0, piece)],
            dst_ref=relay.at[piece_of(0, piece)],
            send_sem=c_send.at[1, piece],
            recv_sem=c_recv.at[1, piece],
            device_id=b_target,
            device_id_type=MESH,
        )

    def c_local(piece):
        return pltpu.make_async_copy(
            result.at[0, piece_of(0, piece)], out_ref.at[piece_of(half, piece)], local_sem.at[piece]
        )

    def g_copy(source, target, step, stage, device):
        return pltpu.make_async_remote_copy(
            src_ref=source,
            dst_ref=target,
            send_sem=g_send.at[step, stage],
            recv_sem=g_recv.at[step, stage],
            device_id=device,
            device_id_type=MESH,
        )

    def each_chunk(body, low=0, high=chunks):
        lax.fori_loop(low, high, lambda chunk, carry: (body(chunk), carry)[1], 0)

    own = pltpu.make_async_copy(
        matrix_ref.at[pl.ds(pl.multiple_of(half * half_rows, CHUNK), half_rows)], first.at[odd], own_sem
    )
    each_chunk(lambda chunk: (a_copy(chunk).start(), r_copy(0, chunk).start()), 0, WINDOW)
    own.start()
    flag_copy = pltpu.make_async_copy(active_ref, flags, flag_sem)
    flag_copy.start()

    def clear():
        gram[...] = jnp.zeros_like(gram)
        norms[...] = jnp.zeros_like(norms)

    def add_gram(held, chunk):
        upper = held[0, rows_of(0, chunk)]
        lower = held[1, rows_of(0, chunk)]
        gram[...] += lax.dot_general(
            jnp.concatenate(split(upper), axis=1),
            jnp.concatenate(split(lower), axis=1),
            (((0,), (0,)), ((), ())),
            preferred_element_type=jnp.float32,
        )
        norms[0] += jnp.sum((upper * upper).reshape(CHUNK // 8, 8, width), axis=0)
        norms[1] += jnp.sum((lower * lower).reshape(CHUNK // 8, 8, width), axis=0)

    def share_gram(step):
        middle = width // 2
        cross = (gram[:width, :width] + gram[width:, width:]) + (gram[:width, width:] + gram[width:, :width])
        for part in range(2):
            partial[step, part, :middle] = cross[part * middle : (part + 1) * middle]
            partial[step, part, middle:] = norms[part]
        copy = g_copy(partial.at[step, 1 - core], arrived.at[step, 0], step, 0, sibling)
        copy.start()
        copy.wait()
        summed[step] = partial[step, core] + arrived[step, 0]
        copies = [
            g_copy(summed.at[step], arrived.at[step, stage], step, stage, device)
            for stage, device in ((1, partner), (2, beside), (3, across))
        ]
        for copy in copies:
            copy.start()
        for copy in copies:
            copy.wait()
        shared[step, core] = (summed[step] + arrived[step, 1]) + (arrived[step, 2] + arrived[step, 3])
        copy = g_copy(shared.at[step, core], shared.at[step, core], step, 4, sibling)
        copy.start()
        copy.wait()
    def make_rotor(step):
        middle = width // 2
        flag = flags[step, pair].astype(jnp.float32)
        cross = jnp.concatenate([shared[step, 0, :middle], shared[step, 1, :middle]], axis=0)
        rotor = rotor_of(cross, shared[step, 0, middle:], shared[step, 1, middle:], flag, total_rows)
        return rotor

    def stack(parts, value):
        high, low = split(value)
        parts[: 2 * width] = high
        parts[2 * width : 4 * width] = high
        parts[4 * width :] = low

    def paired(held, chunk):
        high, low = split(jnp.concatenate([held[0, rows_of(0, chunk)], held[1, rows_of(0, chunk)]], axis=1))
        return jnp.concatenate([high, low, high], axis=1)

    def turned(held, chunk, parts):
        return jnp.dot(paired(held, chunk), parts, preferred_element_type=jnp.float32)

    clear()
    own.wait()
    flag_copy.wait()

    def gather_first(chunk):
        a_copy(chunk).wait_recv()
        even, place = lax.rem(chunk, 2) == 0, chunk // 2

        @pl.when(even)
        def _():
            r_copy(1, place).start()

        @pl.when(jnp.logical_not(even) & (place + WINDOW < ahead_out))
        def _():
            r_copy(0, place + WINDOW).start()

        @pl.when(chunk + WINDOW < chunks)
        def _():
            a_copy(chunk + WINDOW).start()

        add_gram(first, chunk)

    each_chunk(gather_first)
    each_chunk(lambda chunk: r_copy(1, chunk).start(), chunks // 2, ahead_out)
    share_gram(0)
    rotor = make_rotor(0)
    rotor_out[...] = rotor[:, width:]
    h_copy().start()
    stack(rotor_parts, rotor)

    def turn_first(chunk):
        value = turned(first, chunk, rotor_parts[...])
        sending[rows_of(0, chunk)] = value[:, width:]
        second[1, rows_of(0, chunk)] = value[:, :width]

    def turn_upper(chunk):
        second[1, rows_of(0, chunk)] = turned(first, chunk, rotor_parts[:, :width])

    each_chunk(turn_first, ahead_out)
    each_chunk(turn_upper, 0, ahead_out)
    clear()
    each_chunk(lambda chunk: b_copy(chunk).start(), ahead_out)
    h_copy().wait_recv()
    stack(raw_parts, rotor_in[...])

    def turn_raw(chunk):
        r_copy(0, chunk).wait_recv()
        r_copy(1, chunk).wait_recv()
        second[0, rows_of(0, chunk)] = turned(raw, chunk, raw_parts[...])
        add_gram(second, chunk)

    def gather_second(chunk):
        b_copy(chunk).wait_recv()
        add_gram(second, chunk)

    each_chunk(turn_raw, 0, ahead_in)
    each_chunk(gather_second, ahead_in)
    share_gram(1)
    stack(rotor_parts, make_rotor(1))

    def turn_second(chunk):
        value = turned(second, chunk, rotor_parts[...])
        result[1, rows_of(0, chunk)] = value[:, width:]
        result[0, rows_of(0, chunk)] = value[:, :width]
        low, high = chunk * (CHUNK // PIECE), (chunk + 1) * (CHUNK // PIECE)

        @pl.when(high <= FLIGHT)
        def _():
            each_chunk(begin, low, high)

        @pl.when(odd == 1)
        def _():
            each_chunk(lambda piece: c_local(piece).start(), low, high)

    def begin(piece):
        @pl.when(odd == 0)
        def _():
            c_relay(piece).start()
            c_upper(piece).start()

        @pl.when(odd == 1)
        def _():
            c_lower(piece).start()

    each_chunk(turn_second)
    pieces = half_rows // PIECE

    def pace(piece):
        @pl.when(odd == 0)
        def _():
            c_upper(piece).wait_send()

        @pl.when(odd == 1)
        def _():
            c_relay(piece).wait_recv()
            c_passed(piece).start()

        c_lower(piece).wait_send()

        @pl.when(piece + FLIGHT < pieces)
        def _():
            begin(piece + FLIGHT)

    each_chunk(pace, 0, pieces)

    def finish(piece):
        c_upper(piece).wait_recv()

        @pl.when(odd == 0)
        def _():
            c_lower(piece).wait_recv()

        @pl.when(odd == 1)
        def _():
            c_passed(piece).wait_send()
            c_local(piece).wait()

    each_chunk(finish, 0, pieces)
    h_copy().wait_send()
    each_chunk(lambda chunk: b_copy(chunk).wait_send(), ahead_out)
    each_chunk(lambda chunk: (r_copy(0, chunk).wait_send(), r_copy(1, chunk).wait_send()), 0, ahead_out)
    each_chunk(lambda chunk: a_copy(chunk).wait_send())


def solution(mesh):
    col_count = mesh.shape["col"]

    def on_device(matrix, active):
        rows, width = matrix.shape
        half_rows = rows // 2
        chunks = half_rows // CHUNK
        total_rows = rows * mesh.shape["row"]
        payload = width // 2 + TILE
        dma = pltpu.SemaphoreType.DMA
        return pl.pallas_call(
            functools.partial(kernel, total_rows, col_count),
            out_shape=jax.ShapeDtypeStruct(matrix.shape, jnp.float32),
            in_specs=[pl.BlockSpec(memory_space=pl.ANY)] * 2,
            out_specs=pl.BlockSpec(memory_space=pl.ANY),
            scratch_shapes=[
                pltpu.VMEM((2, half_rows, width), jnp.float32),
                pltpu.VMEM((2, AHEAD * CHUNK, width), jnp.float32),
                pltpu.VMEM((2, half_rows, width), jnp.float32),
                pltpu.VMEM((half_rows, width), jnp.float32),
                pltpu.VMEM((2, half_rows, width), jnp.float32),
                pltpu.VMEM((half_rows, width), jnp.float32),
                pltpu.VMEM((2 * width, 2 * width), jnp.float32),
                pltpu.VMEM((2, 8, width), jnp.float32),
                pltpu.VMEM((2, 2, payload, width), jnp.float32),
                pltpu.VMEM((2, 4, payload, width), jnp.float32),
                pltpu.VMEM((2, payload, width), jnp.float32),
                pltpu.VMEM((2, 2, payload, width), jnp.float32),
                pltpu.VMEM((6 * width, 2 * width), jnp.bfloat16),
                pltpu.VMEM((6 * width, width), jnp.bfloat16),
                pltpu.VMEM((2 * width, width), jnp.float32),
                pltpu.VMEM((2 * width, width), jnp.float32),
                pltpu.SMEM(active.shape, jnp.int32),
                dma(()),
                dma(()),
                dma((chunks,)),
                dma((chunks,)),
                dma((2, AHEAD)),
                dma((2, AHEAD)),
                dma(()),
                dma(()),
                dma((chunks,)),
                dma((chunks,)),
                dma((2, 5)),
                dma((2, 5)),
                dma((2, half_rows // PIECE)),
                dma((2, half_rows // PIECE)),
                dma((half_rows // PIECE,)),
            ],
            compiler_params=pltpu.CompilerParams(
                collective_id=0, has_side_effects=True, vmem_limit_bytes=50 * 2**20
            ),
            name="tournament",
        )(matrix, active)

    return jax.shard_map(
        on_device, mesh=mesh, in_specs=(P("row", "col"), P()), out_specs=P("row", "col"), check_vma=False
    )
```

```python
import functools
import math

import jax
import jax.numpy as jnp
from jax import lax
from jax.experimental import pallas as pl
from jax.experimental.pallas import tpu as pltpu
from jax.sharding import PartitionSpec as P

MESH = pl.DeviceIdType.MESH
CHUNK = 256
TILE = 8
AHEAD = 7
SHORT = 5
PIECE = 256
WINDOW = 3
FLIGHT = 4


def lane_spread(value, lane):
    return jnp.broadcast_to(value[:, lane : lane + 1], value.shape)


def eliminate(tiles, block):
    size = TILE
    first = size * block
    shape = tiles[0].shape
    lane = lax.broadcasted_iota(jnp.int32, shape, 1)
    row = lax.broadcasted_iota(jnp.int32, shape, 0)
    inside = (lane >= first) & (lane < first + size)
    rows = [jnp.broadcast_to(tiles[block][i : i + 1], shape) for i in range(size)]
    small = {(i, j): lane_spread(rows[i], first + j) for i in range(size) for j in range(i, size)}
    rows = [jnp.where(inside, jnp.where(lane == first + i, 1.0, 0.0), rows[i]) for i in range(size)]
    inverse, ratio = [None] * size, {}
    for i in range(size):
        if i % 2 == 0:
            head, side, tail = small[i, i], small[i, i + 1], small[i + 1, i + 1]
            inverse[i] = 1.0 / head
            inverse[i + 1] = head * (1.0 / (head * tail - side * side))
        for k in range(i + 1, size):
            ratio[i, k] = small[i, k] * inverse[i]
            for j in range(k, size):
                small[k, j] = small[k, j] - ratio[i, k] * small[i, j]
            rows[k] = rows[k] - ratio[i, k] * rows[i]
    for i in reversed(range(size)):
        rows[i] = rows[i] * inverse[i]
        for k in range(i + 1, size):
            rows[i] = rows[i] - ratio[i, k] * rows[k]
    result = list(tiles)
    for other in range(len(tiles)):
        if other != block:
            value = jnp.where(inside, 0.0, tiles[other])
            spread = [lane_spread(tiles[other], first + i) for i in range(size)]
            upper = value - spread[7] * rows[7] - spread[6] * rows[6]
            lower = spread[5] * rows[5] + spread[4] * rows[4]
            early = spread[3] * rows[3] + spread[2] * rows[2]
            late = spread[1] * rows[1] + spread[0] * rows[0]
            result[other] = (upper - lower) - (early + late)
    solved = rows[0]
    for i in range(1, size):
        solved = jnp.where(row == i, rows[i], solved)
    result[block] = solved
    return result


def inverse_spd(matrix_in):
    order = matrix_in.shape[0]
    tiles = [matrix_in[i : i + TILE] for i in range(0, order, TILE)]
    for block in range(order // TILE):
        tiles = eliminate(tiles, block)
    return jnp.concatenate(tiles, axis=0)


def split(value):
    high = value.astype(jnp.bfloat16)
    return high, (value - high.astype(jnp.float32)).astype(jnp.bfloat16)


def exact_dot(left, right, left_dim=1, right_dim=0):
    return lax.dot_general(
        left,
        right,
        (((left_dim,), (right_dim,)), ((), ())),
        precision=lax.Precision.HIGHEST,
        preferred_element_type=jnp.float32,
    )


def rotor_of(cross, norm_upper, norm_lower, flag, total_rows):
    width = cross.shape[1]
    scale_upper = 1.0 / jnp.sqrt(jnp.sum(norm_upper, axis=0, keepdims=True) / total_rows + 1e-06)
    scale_lower = 1.0 / jnp.sqrt(jnp.sum(norm_lower, axis=0, keepdims=True) / total_rows + 1e-06)
    scale_rows = jnp.broadcast_to(scale_upper, (width, width)).T
    coupling = 0.25 / math.sqrt(total_rows * width) * flag * scale_rows * cross * scale_lower
    row = lax.broadcasted_iota(jnp.int32, (width, width), 0)
    lane = lax.broadcasted_iota(jnp.int32, (width, width), 1)
    identity = jnp.where(row == lane, 1.0, 0.0)
    inv_left = inverse_spd(identity + exact_dot(coupling, coupling, 1, 1))
    product = exact_dot(inv_left, coupling)
    lower_right = identity - 2.0 * exact_dot(coupling, product, 0, 0)
    top = jnp.concatenate([2.0 * inv_left - identity, 2.0 * product], axis=1)
    bottom = jnp.concatenate([-2.0 * product.T, lower_right], axis=1)
    return jnp.concatenate([top, bottom], axis=0)


def kernel(
    total_rows, col_count, matrix_ref, active_ref, out_ref,
    first, raw, second, sending, result, relay, gram, norms, partial, arrived, summed, shared, rotor_parts, raw_parts, rotor_out, rotor_in, flags,
    flag_sem, own_sem, a_send, a_recv, r_send, r_recv, h_send, h_recv, b_send, b_recv, g_send, g_recv, c_send, c_recv, local_sem,
):
    col, row = lax.axis_index("col"), lax.axis_index("row")
    odd, core = lax.rem(col, 2), lax.rem(row, 2)
    pair = col // 2
    parity = lax.rem(pair, 2)
    half = lax.rem(odd + parity, 2)
    width = matrix_ref.shape[1]
    half_rows = matrix_ref.shape[0] // 2
    chunks = half_rows // CHUNK
    upper_col = 2 * pair

    def wrapped(position):
        return lax.rem(position + col_count, col_count)

    partner = (col + 1 - 2 * odd, row)
    sibling = (col, row + 1 - 2 * lax.rem(row, 2))
    beside = (col, lax.rem(row + 2, 4))
    across = (col + 1 - 2 * odd, lax.rem(row + 2, 4))
    b_target = (wrapped(upper_col + 3 - odd), row)
    b_source = (wrapped(upper_col - 1 - odd), row)

    barrier = pltpu.get_barrier_semaphore()
    for device in (partner, sibling, beside, across, b_target, b_source):
        pl.semaphore_signal(barrier, inc=1, device_id=device, device_id_type=MESH)
    pl.semaphore_wait(barrier, 6)

    ahead_out = AHEAD - (AHEAD - SHORT) * parity
    ahead_in = SHORT + (AHEAD - SHORT) * parity

    def rows_of(which, chunk, count=1):
        return pl.ds(pl.multiple_of(which * half_rows + chunk * CHUNK, CHUNK), count * CHUNK)

    def a_copy(chunk):
        return pltpu.make_async_remote_copy(
            src_ref=matrix_ref.at[rows_of(1 - half, chunk)],
            dst_ref=first.at[odd, rows_of(0, chunk)],
            send_sem=a_send.at[chunk],
            recv_sem=a_recv.at[chunk],
            device_id=partner,
            device_id_type=MESH,
        )

    def r_copy(side, chunk):
        source = (matrix_ref.at[rows_of(half, chunk)], first.at[1 - odd, rows_of(0, chunk)])[side]
        return pltpu.make_async_remote_copy(
            src_ref=source,
            dst_ref=raw.at[(odd, 1 - odd)[side], rows_of(0, chunk)],
            send_sem=r_send.at[side, chunk],
            recv_sem=r_recv.at[side, chunk],
            device_id=b_target,
            device_id_type=MESH,
        )

    def h_copy():
        return pltpu.make_async_remote_copy(
            src_ref=rotor_out,
            dst_ref=rotor_in,
            send_sem=h_send,
            recv_sem=h_recv,
            device_id=b_target,
            device_id_type=MESH,
        )

    def b_copy(chunk):
        return pltpu.make_async_remote_copy(
            src_ref=sending.at[rows_of(0, chunk)],
            dst_ref=second.at[0, rows_of(0, chunk)],
            send_sem=b_send.at[chunk],
            recv_sem=b_recv.at[chunk],
            device_id=b_target,
            device_id_type=MESH,
        )

    def piece_of(which, piece):
        return pl.ds(pl.multiple_of(which * half_rows + piece * PIECE, PIECE), PIECE)

    def to_output(source, send, recv, piece, device):
        return pltpu.make_async_remote_copy(
            src_ref=source.at[piece_of(0, piece)],
            dst_ref=out_ref.at[piece_of(half, piece)],
            send_sem=send.at[piece],
            recv_sem=recv.at[piece],
            device_id=device,
            device_id_type=MESH,
        )

    def c_upper(piece):
        return to_output(result.at[0], c_send.at[0], c_recv.at[0], piece, partner)

    def c_lower(piece):
        return to_output(result.at[1], c_send.at[1], c_recv.at[1], piece, b_target)

    def c_passed(piece):
        return to_output(relay, c_send.at[0], c_recv.at[0], piece, partner)

    def c_relay(piece):
        return pltpu.make_async_remote_copy(
            src_ref=result.at[1, piece_of(0, piece)],
            dst_ref=relay.at[piece_of(0, piece)],
            send_sem=c_send.at[1, piece],
            recv_sem=c_recv.at[1, piece],
            device_id=b_target,
            device_id_type=MESH,
        )

    def c_local(piece):
        return pltpu.make_async_copy(
            result.at[0, piece_of(0, piece)], out_ref.at[piece_of(half, piece)], local_sem.at[piece]
        )

    def g_copy(source, target, step, stage, device):
        return pltpu.make_async_remote_copy(
            src_ref=source,
            dst_ref=target,
            send_sem=g_send.at[step, stage],
            recv_sem=g_recv.at[step, stage],
            device_id=device,
            device_id_type=MESH,
        )

    def each_chunk(body, low=0, high=chunks):
        lax.fori_loop(low, high, lambda chunk, carry: (body(chunk), carry)[1], 0)

    own = pltpu.make_async_copy(
        matrix_ref.at[pl.ds(pl.multiple_of(half * half_rows, CHUNK), half_rows)], first.at[odd], own_sem
    )
    each_chunk(lambda chunk: (a_copy(chunk).start(), r_copy(0, chunk).start()), 0, WINDOW)
    own.start()
    flag_copy = pltpu.make_async_copy(active_ref, flags, flag_sem)
    flag_copy.start()

    def clear():
        gram[...] = jnp.zeros_like(gram)
        norms[...] = jnp.zeros_like(norms)

    def add_gram(held, chunk, count=1):
        upper = held[0, rows_of(0, chunk, count)]
        lower = held[1, rows_of(0, chunk, count)]
        gram[...] += lax.dot_general(
            jnp.concatenate(split(upper), axis=1),
            jnp.concatenate(split(lower), axis=1),
            (((0,), (0,)), ((), ())),
            preferred_element_type=jnp.float32,
        )
        norms[0] += jnp.sum((upper * upper).reshape(count * CHUNK // 8, 8, width), axis=0)
        norms[1] += jnp.sum((lower * lower).reshape(count * CHUNK // 8, 8, width), axis=0)

    def share_gram(step):
        middle = width // 2
        cross = (gram[:width, :width] + gram[width:, width:]) + (gram[:width, width:] + gram[width:, :width])
        for part in range(2):
            partial[step, part, :middle] = cross[part * middle : (part + 1) * middle]
            partial[step, part, middle:] = norms[part]
        copy = g_copy(partial.at[step, 1 - core], arrived.at[step, 0], step, 0, sibling)
        copy.start()
        copy.wait()
        summed[step] = partial[step, core] + arrived[step, 0]
        copies = [
            g_copy(summed.at[step], arrived.at[step, stage], step, stage, device)
            for stage, device in ((1, partner), (2, beside), (3, across))
        ]
        for copy in copies:
            copy.start()
        for copy in copies:
            copy.wait()
        shared[step, core] = (summed[step] + arrived[step, 1]) + (arrived[step, 2] + arrived[step, 3])
        copy = g_copy(shared.at[step, core], shared.at[step, core], step, 4, sibling)
        copy.start()
        copy.wait()
    def make_rotor(step):
        middle = width // 2
        flag = flags[step, pair].astype(jnp.float32)
        cross = jnp.concatenate([shared[step, 0, :middle], shared[step, 1, :middle]], axis=0)
        rotor = rotor_of(cross, shared[step, 0, middle:], shared[step, 1, middle:], flag, total_rows)
        return rotor

    def stack(parts, value):
        high, low = split(value)
        parts[: 2 * width] = high
        parts[2 * width : 4 * width] = high
        parts[4 * width :] = low

    def paired(held, chunk, count):
        high, low = split(jnp.concatenate([held[0, rows_of(0, chunk, count)], held[1, rows_of(0, chunk, count)]], axis=1))
        return jnp.concatenate([high, low, high], axis=1)

    def turned(held, chunk, parts, count=1):
        return jnp.dot(paired(held, chunk, count), parts, preferred_element_type=jnp.float32)

    clear()
    own.wait()
    flag_copy.wait()

    def gather_first(chunk):
        a_copy(chunk).wait_recv()
        even, place = lax.rem(chunk, 2) == 0, chunk // 2

        @pl.when(even)
        def _():
            r_copy(1, place).start()

        @pl.when(jnp.logical_not(even) & (place + WINDOW < ahead_out))
        def _():
            r_copy(0, place + WINDOW).start()

        @pl.when(chunk + WINDOW < chunks)
        def _():
            a_copy(chunk + WINDOW).start()

        add_gram(first, chunk)

    each_chunk(gather_first)
    each_chunk(lambda chunk: r_copy(1, chunk).start(), chunks // 2, ahead_out)
    share_gram(0)
    rotor = make_rotor(0)
    rotor_out[...] = rotor[:, width:]
    h_copy().start()
    stack(rotor_parts, rotor)

    def turn_first(chunk):
        value = turned(first, chunk, rotor_parts[...])
        sending[rows_of(0, chunk)] = value[:, width:]
        second[1, rows_of(0, chunk)] = value[:, :width]

    def turn_upper(chunk):
        second[1, rows_of(0, chunk)] = turned(first, chunk, rotor_parts[:, :width])

    each_chunk(turn_first, ahead_out)
    each_chunk(turn_upper, 0, ahead_out)
    clear()
    each_chunk(lambda chunk: b_copy(chunk).start(), ahead_out)
    h_copy().wait_recv()
    stack(raw_parts, rotor_in[...])

    def turn_raw(chunk, count=1):
        for place in range(count):
            r_copy(0, chunk + place).wait_recv()
            r_copy(1, chunk + place).wait_recv()
        second[0, rows_of(0, chunk, count)] = turned(raw, chunk, raw_parts[...], count)
        add_gram(second, chunk, count)

    def gather_second(chunk):
        b_copy(chunk).wait_recv()
        add_gram(second, chunk)

    each_chunk(lambda double: turn_raw(2 * double, 2), 0, ahead_in // 2)
    each_chunk(turn_raw, ahead_in // 2 * 2, ahead_in)
    each_chunk(gather_second, ahead_in)
    share_gram(1)
    stack(rotor_parts, make_rotor(1))

    def turn_second(chunk):
        value = turned(second, chunk, rotor_parts[...])
        result[1, rows_of(0, chunk)] = value[:, width:]
        result[0, rows_of(0, chunk)] = value[:, :width]
        low, high = chunk * (CHUNK // PIECE), (chunk + 1) * (CHUNK // PIECE)

        @pl.when(high <= FLIGHT)
        def _():
            each_chunk(begin, low, high)

        @pl.when(odd == 1)
        def _():
            each_chunk(lambda piece: c_local(piece).start(), low, high)

    def begin(piece):
        @pl.when(odd == 0)
        def _():
            c_relay(piece).start()
            c_upper(piece).start()

        @pl.when(odd == 1)
        def _():
            c_lower(piece).start()

    each_chunk(turn_second)
    pieces = half_rows // PIECE

    def pace(piece):
        @pl.when(odd == 0)
        def _():
            c_upper(piece).wait_send()

        @pl.when(odd == 1)
        def _():
            c_relay(piece).wait_recv()
            c_passed(piece).start()

        c_lower(piece).wait_send()

        @pl.when(piece + FLIGHT < pieces)
        def _():
            begin(piece + FLIGHT)

    each_chunk(pace, 0, pieces)

    def finish(piece):
        c_upper(piece).wait_recv()

        @pl.when(odd == 0)
        def _():
            c_lower(piece).wait_recv()

        @pl.when(odd == 1)
        def _():
            c_passed(piece).wait_send()
            c_local(piece).wait()

    each_chunk(finish, 0, pieces)
    h_copy().wait_send()
    each_chunk(lambda chunk: b_copy(chunk).wait_send(), ahead_out)
    each_chunk(lambda chunk: (r_copy(0, chunk).wait_send(), r_copy(1, chunk).wait_send()), 0, ahead_out)
    each_chunk(lambda chunk: a_copy(chunk).wait_send())


def solution(mesh):
    col_count = mesh.shape["col"]

    def on_device(matrix, active):
        rows, width = matrix.shape
        half_rows = rows // 2
        chunks = half_rows // CHUNK
        total_rows = rows * mesh.shape["row"]
        payload = width // 2 + TILE
        dma = pltpu.SemaphoreType.DMA
        return pl.pallas_call(
            functools.partial(kernel, total_rows, col_count),
            out_shape=jax.ShapeDtypeStruct(matrix.shape, jnp.float32),
            in_specs=[pl.BlockSpec(memory_space=pl.ANY)] * 2,
            out_specs=pl.BlockSpec(memory_space=pl.ANY),
            scratch_shapes=[
                pltpu.VMEM((2, half_rows, width), jnp.float32),
                pltpu.VMEM((2, AHEAD * CHUNK, width), jnp.float32),
                pltpu.VMEM((2, half_rows, width), jnp.float32),
                pltpu.VMEM((half_rows, width), jnp.float32),
                pltpu.VMEM((2, half_rows, width), jnp.float32),
                pltpu.VMEM((half_rows, width), jnp.float32),
                pltpu.VMEM((2 * width, 2 * width), jnp.float32),
                pltpu.VMEM((2, 8, width), jnp.float32),
                pltpu.VMEM((2, 2, payload, width), jnp.float32),
                pltpu.VMEM((2, 4, payload, width), jnp.float32),
                pltpu.VMEM((2, payload, width), jnp.float32),
                pltpu.VMEM((2, 2, payload, width), jnp.float32),
                pltpu.VMEM((6 * width, 2 * width), jnp.bfloat16),
                pltpu.VMEM((6 * width, width), jnp.bfloat16),
                pltpu.VMEM((2 * width, width), jnp.float32),
                pltpu.VMEM((2 * width, width), jnp.float32),
                pltpu.SMEM(active.shape, jnp.int32),
                dma(()),
                dma(()),
                dma((chunks,)),
                dma((chunks,)),
                dma((2, AHEAD)),
                dma((2, AHEAD)),
                dma(()),
                dma(()),
                dma((chunks,)),
                dma((chunks,)),
                dma((2, 5)),
                dma((2, 5)),
                dma((2, half_rows // PIECE)),
                dma((2, half_rows // PIECE)),
                dma((half_rows // PIECE,)),
            ],
            compiler_params=pltpu.CompilerParams(
                collective_id=0, has_side_effects=True, vmem_limit_bytes=50 * 2**20
            ),
            name="tournament",
        )(matrix, active)

    return jax.shard_map(
        on_device, mesh=mesh, in_specs=(P("row", "col"), P()), out_specs=P("row", "col"), check_vma=False
    )
```

```python
import functools
import math

import jax
import jax.numpy as jnp
from jax import lax
from jax.experimental import pallas as pl
from jax.experimental.pallas import tpu as pltpu
from jax.sharding import PartitionSpec as P

MESH = pl.DeviceIdType.MESH
CHUNK = 256
TILE = 8
AHEAD = 7
SHORT = 5
PIECE = 256
WINDOW = 3
FLIGHT = 4


def lane_spread(value, lane):
    return jnp.broadcast_to(value[:, lane : lane + 1], value.shape)


def eliminate(tiles, block):
    size = TILE
    first = size * block
    shape = tiles[0].shape
    lane = lax.broadcasted_iota(jnp.int32, shape, 1)
    row = lax.broadcasted_iota(jnp.int32, shape, 0)
    inside = (lane >= first) & (lane < first + size)
    rows = [jnp.broadcast_to(tiles[block][i : i + 1], shape) for i in range(size)]
    small = {(i, j): lane_spread(rows[i], first + j) for i in range(size) for j in range(i, size)}
    rows = [jnp.where(inside, jnp.where(lane == first + i, 1.0, 0.0), rows[i]) for i in range(size)]
    inverse, ratio = [None] * size, {}
    for i in range(size):
        if i % 2 == 0:
            head, side, tail = small[i, i], small[i, i + 1], small[i + 1, i + 1]
            inverse[i] = 1.0 / head
            inverse[i + 1] = head * (1.0 / (head * tail - side * side))
        for k in range(i + 1, size):
            ratio[i, k] = small[i, k] * inverse[i]
            for j in range(k, size):
                small[k, j] = small[k, j] - ratio[i, k] * small[i, j]
            rows[k] = rows[k] - ratio[i, k] * rows[i]
    for i in reversed(range(size)):
        rows[i] = rows[i] * inverse[i]
        for k in range(i + 1, size):
            rows[i] = rows[i] - ratio[i, k] * rows[k]
    result = list(tiles)
    for other in range(len(tiles)):
        if other != block:
            value = jnp.where(inside, 0.0, tiles[other])
            spread = [lane_spread(tiles[other], first + i) for i in range(size)]
            upper = value - spread[7] * rows[7] - spread[6] * rows[6]
            lower = spread[5] * rows[5] + spread[4] * rows[4]
            early = spread[3] * rows[3] + spread[2] * rows[2]
            late = spread[1] * rows[1] + spread[0] * rows[0]
            result[other] = (upper - lower) - (early + late)
    solved = rows[0]
    for i in range(1, size):
        solved = jnp.where(row == i, rows[i], solved)
    result[block] = solved
    return result


def inverse_spd(matrix_in):
    order = matrix_in.shape[0]
    tiles = [matrix_in[i : i + TILE] for i in range(0, order, TILE)]
    for block in range(order // TILE):
        tiles = eliminate(tiles, block)
    return jnp.concatenate(tiles, axis=0)


def split(value):
    high = value.astype(jnp.bfloat16)
    return high, (value - high.astype(jnp.float32)).astype(jnp.bfloat16)


def exact_dot(left, right, left_dim=1, right_dim=0):
    return lax.dot_general(
        left,
        right,
        (((left_dim,), (right_dim,)), ((), ())),
        precision=lax.Precision.HIGHEST,
        preferred_element_type=jnp.float32,
    )


def rotor_of(cross, norm_upper, norm_lower, flag, total_rows):
    width = cross.shape[1]
    scale_upper = 1.0 / jnp.sqrt(jnp.sum(norm_upper, axis=0, keepdims=True) / total_rows + 1e-06)
    scale_lower = 1.0 / jnp.sqrt(jnp.sum(norm_lower, axis=0, keepdims=True) / total_rows + 1e-06)
    scale_rows = jnp.broadcast_to(scale_upper, (width, width)).T
    coupling = 0.25 / math.sqrt(total_rows * width) * flag * scale_rows * cross * scale_lower
    row = lax.broadcasted_iota(jnp.int32, (width, width), 0)
    lane = lax.broadcasted_iota(jnp.int32, (width, width), 1)
    identity = jnp.where(row == lane, 1.0, 0.0)
    inv_left = inverse_spd(identity + exact_dot(coupling, coupling, 1, 1))
    product = exact_dot(inv_left, coupling)
    lower_right = identity - 2.0 * exact_dot(coupling, product, 0, 0)
    top = jnp.concatenate([2.0 * inv_left - identity, 2.0 * product], axis=1)
    bottom = jnp.concatenate([-2.0 * product.T, lower_right], axis=1)
    return jnp.concatenate([top, bottom], axis=0)


def kernel(
    total_rows, col_count, matrix_ref, active_ref, out_ref,
    first, raw, second, sending, result, relay, gram, norms, partial, arrived, summed, shared, rotor_parts, raw_parts, rotor_out, rotor_in, flags,
    flag_sem, own_sem, a_send, a_recv, r_send, r_recv, h_send, h_recv, b_send, b_recv, g_send, g_recv, c_send, c_recv, local_sem,
):
    col, row = lax.axis_index("col"), lax.axis_index("row")
    odd, core = lax.rem(col, 2), lax.rem(row, 2)
    pair = col // 2
    parity = lax.rem(pair, 2)
    half = lax.rem(odd + parity, 2)
    width = matrix_ref.shape[1]
    half_rows = matrix_ref.shape[0] // 2
    chunks = half_rows // CHUNK
    upper_col = 2 * pair

    def wrapped(position):
        return lax.rem(position + col_count, col_count)

    partner = (col + 1 - 2 * odd, row)
    sibling = (col, row + 1 - 2 * lax.rem(row, 2))
    beside = (col, lax.rem(row + 2, 4))
    across = (col + 1 - 2 * odd, lax.rem(row + 2, 4))
    b_target = (wrapped(upper_col + 3 - odd), row)
    b_source = (wrapped(upper_col - 1 - odd), row)

    barrier = pltpu.get_barrier_semaphore()
    for device in (partner, sibling, beside, across, b_target, b_source):
        pl.semaphore_signal(barrier, inc=1, device_id=device, device_id_type=MESH)
    pl.semaphore_wait(barrier, 6)

    ahead_out = AHEAD - (AHEAD - SHORT) * parity
    ahead_in = SHORT + (AHEAD - SHORT) * parity

    def rows_of(which, chunk, count=1):
        return pl.ds(pl.multiple_of(which * half_rows + chunk * CHUNK, CHUNK), count * CHUNK)

    def a_copy(chunk):
        return pltpu.make_async_remote_copy(
            src_ref=matrix_ref.at[rows_of(1 - half, chunk)],
            dst_ref=first.at[odd, rows_of(0, chunk)],
            send_sem=a_send.at[chunk],
            recv_sem=a_recv.at[chunk],
            device_id=partner,
            device_id_type=MESH,
        )

    def r_copy(side, chunk):
        source = (matrix_ref.at[rows_of(half, chunk)], first.at[1 - odd, rows_of(0, chunk)])[side]
        return pltpu.make_async_remote_copy(
            src_ref=source,
            dst_ref=raw.at[(odd, 1 - odd)[side], rows_of(0, chunk)],
            send_sem=r_send.at[side, chunk],
            recv_sem=r_recv.at[side, chunk],
            device_id=b_target,
            device_id_type=MESH,
        )

    def h_copy():
        return pltpu.make_async_remote_copy(
            src_ref=rotor_out,
            dst_ref=rotor_in,
            send_sem=h_send,
            recv_sem=h_recv,
            device_id=b_target,
            device_id_type=MESH,
        )

    def b_copy(chunk):
        return pltpu.make_async_remote_copy(
            src_ref=sending.at[rows_of(0, chunk)],
            dst_ref=second.at[0, rows_of(0, chunk)],
            send_sem=b_send.at[chunk],
            recv_sem=b_recv.at[chunk],
            device_id=b_target,
            device_id_type=MESH,
        )

    def piece_of(which, piece):
        return pl.ds(pl.multiple_of(which * half_rows + piece * PIECE, PIECE), PIECE)

    def to_output(source, send, recv, piece, device):
        return pltpu.make_async_remote_copy(
            src_ref=source.at[piece_of(0, piece)],
            dst_ref=out_ref.at[piece_of(half, piece)],
            send_sem=send.at[piece],
            recv_sem=recv.at[piece],
            device_id=device,
            device_id_type=MESH,
        )

    def c_upper(piece):
        return to_output(result.at[0], c_send.at[0], c_recv.at[0], piece, partner)

    def c_lower(piece):
        return to_output(result.at[1], c_send.at[1], c_recv.at[1], piece, b_target)

    def c_passed(piece):
        return to_output(relay, c_send.at[0], c_recv.at[0], piece, partner)

    def c_relay(piece):
        return pltpu.make_async_remote_copy(
            src_ref=result.at[1, piece_of(0, piece)],
            dst_ref=relay.at[piece_of(0, piece)],
            send_sem=c_send.at[1, piece],
            recv_sem=c_recv.at[1, piece],
            device_id=b_target,
            device_id_type=MESH,
        )

    def c_local(piece):
        return pltpu.make_async_copy(
            result.at[0, piece_of(0, piece)], out_ref.at[piece_of(half, piece)], local_sem.at[piece]
        )

    def g_copy(source, target, step, stage, device):
        return pltpu.make_async_remote_copy(
            src_ref=source,
            dst_ref=target,
            send_sem=g_send.at[step, stage],
            recv_sem=g_recv.at[step, stage],
            device_id=device,
            device_id_type=MESH,
        )

    def each_chunk(body, low=0, high=chunks):
        lax.fori_loop(low, high, lambda chunk, carry: (body(chunk), carry)[1], 0)

    own = pltpu.make_async_copy(
        matrix_ref.at[pl.ds(pl.multiple_of(half * half_rows, CHUNK), half_rows)], first.at[odd], own_sem
    )
    each_chunk(lambda chunk: (a_copy(chunk).start(), r_copy(0, chunk).start()), 0, WINDOW)
    own.start()
    flag_copy = pltpu.make_async_copy(active_ref, flags, flag_sem)
    flag_copy.start()

    def clear():
        gram[...] = jnp.zeros_like(gram)
        norms[...] = jnp.zeros_like(norms)

    def add_gram(held, chunk, count=1):
        upper = held[0, rows_of(0, chunk, count)]
        lower = held[1, rows_of(0, chunk, count)]
        gram[...] += lax.dot_general(
            jnp.concatenate(split(upper), axis=1),
            jnp.concatenate(split(lower), axis=1),
            (((0,), (0,)), ((), ())),
            preferred_element_type=jnp.float32,
        )
        norms[0] += jnp.sum((upper * upper).reshape(count * CHUNK // 8, 8, width), axis=0)
        norms[1] += jnp.sum((lower * lower).reshape(count * CHUNK // 8, 8, width), axis=0)

    def share_gram(step):
        middle = width // 2
        cross = (gram[:width, :width] + gram[width:, width:]) + (gram[:width, width:] + gram[width:, :width])
        for part in range(2):
            partial[step, part, :middle] = cross[part * middle : (part + 1) * middle]
            partial[step, part, middle:] = norms[part]
        copy = g_copy(partial.at[step, 1 - core], arrived.at[step, 0], step, 0, sibling)
        copy.start()
        copy.wait()
        summed[step] = partial[step, core] + arrived[step, 0]
        copies = [
            g_copy(summed.at[step], arrived.at[step, stage], step, stage, device)
            for stage, device in ((1, partner), (2, beside), (3, across))
        ]
        for copy in copies:
            copy.start()
        for copy in copies:
            copy.wait()
        shared[step, core] = (summed[step] + arrived[step, 1]) + (arrived[step, 2] + arrived[step, 3])
        copy = g_copy(shared.at[step, core], shared.at[step, core], step, 4, sibling)
        copy.start()
        copy.wait()
    def make_rotor(step):
        middle = width // 2
        flag = flags[step, pair].astype(jnp.float32)
        cross = jnp.concatenate([shared[step, 0, :middle], shared[step, 1, :middle]], axis=0)
        rotor = rotor_of(cross, shared[step, 0, middle:], shared[step, 1, middle:], flag, total_rows)
        return rotor

    def stack(parts, value):
        high, low = split(value)
        parts[: 2 * width] = high
        parts[2 * width : 4 * width] = high
        parts[4 * width :] = low

    def paired(held, chunk, count):
        high, low = split(jnp.concatenate([held[0, rows_of(0, chunk, count)], held[1, rows_of(0, chunk, count)]], axis=1))
        return jnp.concatenate([high, low, high], axis=1)

    def turned(held, chunk, parts, count=1):
        return jnp.dot(paired(held, chunk, count), parts, preferred_element_type=jnp.float32)

    clear()
    own.wait()
    flag_copy.wait()

    def gather_first(chunk):
        a_copy(chunk).wait_recv()
        even, place = lax.rem(chunk, 2) == 0, chunk // 2

        @pl.when(even)
        def _():
            r_copy(1, place).start()

        @pl.when(jnp.logical_not(even) & (place + WINDOW < ahead_out))
        def _():
            r_copy(0, place + WINDOW).start()

        @pl.when(chunk + WINDOW < chunks)
        def _():
            a_copy(chunk + WINDOW).start()

        add_gram(first, chunk)

    each_chunk(gather_first)
    each_chunk(lambda chunk: r_copy(1, chunk).start(), chunks // 2, ahead_out)
    share_gram(0)
    rotor = make_rotor(0)
    rotor_out[...] = rotor[:, width:]
    h_copy().start()
    stack(rotor_parts, rotor)

    def turn_first(chunk):
        value = turned(first, chunk, rotor_parts[...])
        sending[rows_of(0, chunk)] = value[:, width:]
        second[1, rows_of(0, chunk)] = value[:, :width]

    def turn_upper(chunk, count=1):
        second[1, rows_of(0, chunk, count)] = turned(first, chunk, rotor_parts[:, :width], count)

    each_chunk(turn_first, ahead_out)
    each_chunk(lambda double: turn_upper(2 * double, 2), 0, ahead_out // 2)
    each_chunk(turn_upper, ahead_out // 2 * 2, ahead_out)
    clear()
    each_chunk(lambda chunk: b_copy(chunk).start(), ahead_out)
    h_copy().wait_recv()
    stack(raw_parts, rotor_in[...])

    def turn_raw(chunk, count=1):
        for place in range(count):
            r_copy(0, chunk + place).wait_recv()
            r_copy(1, chunk + place).wait_recv()
        second[0, rows_of(0, chunk, count)] = turned(raw, chunk, raw_parts[...], count)
        add_gram(second, chunk, count)

    def gather_second(chunk):
        b_copy(chunk).wait_recv()
        add_gram(second, chunk)

    each_chunk(lambda double: turn_raw(2 * double, 2), 0, ahead_in // 2)
    each_chunk(turn_raw, ahead_in // 2 * 2, ahead_in)
    each_chunk(gather_second, ahead_in)
    share_gram(1)
    stack(rotor_parts, make_rotor(1))

    def turn_second(chunk):
        value = turned(second, chunk, rotor_parts[...])
        result[1, rows_of(0, chunk)] = value[:, width:]
        result[0, rows_of(0, chunk)] = value[:, :width]
        low, high = chunk * (CHUNK // PIECE), (chunk + 1) * (CHUNK // PIECE)

        @pl.when(high <= FLIGHT)
        def _():
            each_chunk(begin, low, high)

        @pl.when(odd == 1)
        def _():
            each_chunk(lambda piece: c_local(piece).start(), low, high)

    def begin(piece):
        @pl.when(odd == 0)
        def _():
            c_relay(piece).start()
            c_upper(piece).start()

        @pl.when(odd == 1)
        def _():
            c_lower(piece).start()

    each_chunk(turn_second)
    pieces = half_rows // PIECE

    def pace(piece):
        @pl.when(odd == 0)
        def _():
            c_upper(piece).wait_send()

        @pl.when(odd == 1)
        def _():
            c_relay(piece).wait_recv()
            c_passed(piece).start()

        c_lower(piece).wait_send()

        @pl.when(piece + FLIGHT < pieces)
        def _():
            begin(piece + FLIGHT)

    each_chunk(pace, 0, pieces)

    def finish(piece):
        c_upper(piece).wait_recv()

        @pl.when(odd == 0)
        def _():
            c_lower(piece).wait_recv()

        @pl.when(odd == 1)
        def _():
            c_passed(piece).wait_send()
            c_local(piece).wait()

    each_chunk(finish, 0, pieces)
    h_copy().wait_send()
    each_chunk(lambda chunk: b_copy(chunk).wait_send(), ahead_out)
    each_chunk(lambda chunk: (r_copy(0, chunk).wait_send(), r_copy(1, chunk).wait_send()), 0, ahead_out)
    each_chunk(lambda chunk: a_copy(chunk).wait_send())


def solution(mesh):
    col_count = mesh.shape["col"]

    def on_device(matrix, active):
        rows, width = matrix.shape
        half_rows = rows // 2
        chunks = half_rows // CHUNK
        total_rows = rows * mesh.shape["row"]
        payload = width // 2 + TILE
        dma = pltpu.SemaphoreType.DMA
        return pl.pallas_call(
            functools.partial(kernel, total_rows, col_count),
            out_shape=jax.ShapeDtypeStruct(matrix.shape, jnp.float32),
            in_specs=[pl.BlockSpec(memory_space=pl.ANY)] * 2,
            out_specs=pl.BlockSpec(memory_space=pl.ANY),
            scratch_shapes=[
                pltpu.VMEM((2, half_rows, width), jnp.float32),
                pltpu.VMEM((2, AHEAD * CHUNK, width), jnp.float32),
                pltpu.VMEM((2, half_rows, width), jnp.float32),
                pltpu.VMEM((half_rows, width), jnp.float32),
                pltpu.VMEM((2, half_rows, width), jnp.float32),
                pltpu.VMEM((half_rows, width), jnp.float32),
                pltpu.VMEM((2 * width, 2 * width), jnp.float32),
                pltpu.VMEM((2, 8, width), jnp.float32),
                pltpu.VMEM((2, 2, payload, width), jnp.float32),
                pltpu.VMEM((2, 4, payload, width), jnp.float32),
                pltpu.VMEM((2, payload, width), jnp.float32),
                pltpu.VMEM((2, 2, payload, width), jnp.float32),
                pltpu.VMEM((6 * width, 2 * width), jnp.bfloat16),
                pltpu.VMEM((6 * width, width), jnp.bfloat16),
                pltpu.VMEM((2 * width, width), jnp.float32),
                pltpu.VMEM((2 * width, width), jnp.float32),
                pltpu.SMEM(active.shape, jnp.int32),
                dma(()),
                dma(()),
                dma((chunks,)),
                dma((chunks,)),
                dma((2, AHEAD)),
                dma((2, AHEAD)),
                dma(()),
                dma(()),
                dma((chunks,)),
                dma((chunks,)),
                dma((2, 5)),
                dma((2, 5)),
                dma((2, half_rows // PIECE)),
                dma((2, half_rows // PIECE)),
                dma((half_rows // PIECE,)),
            ],
            compiler_params=pltpu.CompilerParams(
                collective_id=0, has_side_effects=True, vmem_limit_bytes=50 * 2**20
            ),
            name="tournament",
        )(matrix, active)

    return jax.shard_map(
        on_device, mesh=mesh, in_specs=(P("row", "col"), P()), out_specs=P("row", "col"), check_vma=False
    )
```
